256 devices in a mesh: seq: 16 (over y, z_hi), tp: 4 (over x), dp: 4 (over z_lo, core).
Axes of the slice: x: 4, y: 4, z: 8 (z_hi: 4, z_lo: 2; z = z_hi * 2 + z_lo), core: 2. Of those that a mesh axis runs over, the one named last changes fastest.
Arguments:
- seq_input: bfloat16 [4, 16384, 8192], P('tp', 'seq', 'dp'), may hold values from -4 to 4
- seq_b: bfloat16 [4, 16384, 1024], P('tp', 'seq', 'dp'), may hold values from -0.5 to 0.5
- seq_c: bfloat16 [4, 16384, 1024], P('tp', 'seq', 'dp'), may hold values from -0.5 to 0.5
- seq_decay: float32 [4, 128, 16384], P('tp', 'dp', 'seq'), may hold values from -1 to 0, as said below
- row_prompt: int32 [256], P(('seq', 'dp')), may hold values from 0 to 3
- cache_slot: int32 [256], P(('seq', 'dp')), may hold values from 0 to 3, as said below
- step_input: bfloat16 [8, 256, 8192], P(None, ('seq', 'dp'), 'tp'), may hold values from -8 to 8
- step_b: bfloat16 [8, 256, 1024], P(None, ('seq', 'dp'), 'tp'), may hold values from -0.5 to 0.5
- step_c: bfloat16 [8, 256, 1024], P(None, ('seq', 'dp'), 'tp'), may hold values from -0.5 to 0.5
- step_decay: float32 [8, 256, 128], P(None, ('seq', 'dp'), 'tp'), may hold values from 0.5 to 1
Outputs:
- seq_output: bfloat16 [4, 16384, 8192], P('tp', 'seq', 'dp')
- step_output: bfloat16 [8, 256, 8192], P(None, ('seq', 'dp'), 'tp')
- state_cache: bfloat16 [256, 128, 64, 128], P(('seq', 'dp'), 'tp')
The draws below stay inside these ranges and needn't reach their ends.
Inputs may be any that keep to these rules, and one draw needn't show every extreme that they name: `seq_decay`: every entry is negative. `cache_slot`: each aligned block of 4 rows holds each of 0 to 3 once.
All inputs are finite; a program needn't handle non-finite values.
Results may differ from the reference program's by a relative error of at most 0.0055.
Values sent between devices are 32-bit elements; how exact they have to be, the bound alone decides.
A program may use at most 128 MiB of HBM per device.

```python
import math
import jax
import jax.numpy as jnp
from jax import lax

H = 128
P_SIZE = 64
N = 128
G = 8
Q = 256
L_DEV = 1024
R_DEV = 4
STEPS = 8
PROMPTS = 4
PROMPT_LENGTH = 16384
ROWS = 256


def head_decay_rates(key, slow_share, fastest):
    first, second, third = jax.random.split(key, 3)
    slow = jax.random.uniform(first, (H,)) < slow_share
    fast_rate = jnp.exp(jax.random.uniform(second, (H,), minval=math.log(1.0 / 240.0), maxval=math.log(fastest)))
    slow_rate = jnp.exp(jax.random.uniform(third, (H,), minval=math.log(0.05), maxval=0.0)) * (0.8 / PROMPT_LENGTH)
    return jnp.where(slow, slow_rate, fast_rate)


def draw_seq_decay(key, part):
    key = jax.random.fold_in(key, 3)
    forgetting_factors = head_decay_rates(jax.random.fold_in(key, 17), 0.5, 1.0 / 30.0)
    first, second, third, fourth = jax.random.split(key, 4)
    symbol_element = jnp.exp(jax.random.uniform(first, (PROMPTS, H, PROMPT_LENGTH), minval=math.log(0.5), maxval=math.log(1.5)))
    segment_array = jnp.exp(jax.random.uniform(second, (PROMPTS, H, PROMPT_LENGTH // L_DEV, 1), minval=math.log(0.5), maxval=math.log(2.0)))
    segment_array = jnp.broadcast_to(segment_array, (PROMPTS, H, PROMPT_LENGTH // L_DEV, L_DEV)).reshape(PROMPTS, H, PROMPT_LENGTH)
    places = jax.random.randint(third, (PROMPTS, 1, 3), 0, PROMPT_LENGTH)
    agreement_tally = jnp.any(jnp.arange(PROMPT_LENGTH, dtype=jnp.int32)[None, :, None] == places, axis=-1)
    mismatch_measure = jax.random.uniform(fourth, (PROMPTS, H, 1), minval=0.2, maxval=0.5)
    cluster_of_channels = jnp.where(agreement_tally[:, None, :], jnp.log(1.0 - mismatch_measure), 0.0)
    return (-forgetting_factors[None, :, None] * symbol_element * segment_array + cluster_of_channels).astype(jnp.float32)


def draw_cache_slot(key, part):
    key = jax.random.fold_in(key, 5)
    keys = jax.random.split(key, ROWS // R_DEV)
    orders = jax.vmap(lambda single_token_row: jax.random.permutation(single_token_row, R_DEV))(keys)
    return orders.reshape(ROWS).astype(jnp.int32)


def set_ends(entries, key, least, high):
    index_at = [jax.random.randint(jax.random.fold_in(key, axis), (), 0, length) for axis, length in enumerate(entries.shape)]
    longest = entries.shape.index(max(entries.shape))
    next_to = index_at[:longest] + [(index_at[longest] + 1) % entries.shape[longest]] + index_at[longest + 1:]
    return entries.at[tuple(index_at)].set(least).at[tuple(next_to)].set(high)


def block_scale(own_key, shape, cuts, low, high):
    gain, own = 1.0, jax.random.fold_in(own_key, 6)
    for dim, shards_of in cuts:
        heights = jnp.exp(jax.random.uniform(jax.random.fold_in(own, dim), (shards_of,), jnp.float32, low / len(cuts), high / len(cuts)))
        gain = gain * jnp.repeat(heights, shape[dim] // shards_of).reshape([-1 if axis == dim else 1 for axis in range(len(shape))])
    return gain


def centred(own_key, dims, spread, bound, pieces=(), kind=jnp.bfloat16):
    drawn = spread * jax.random.normal(own_key, dims, jnp.float32)
    if pieces:
        drawn = drawn * block_scale(own_key, dims, pieces, -0.22, 0.18)
    return jnp.clip(drawn, -bound, bound).astype(kind)


def setup_inputs(seed: int = 0) -> dict:
    seeds = jax.random.split(jax.random.key(seed), 11)
    seq_input = centred(seeds[0], (PROMPTS, PROMPT_LENGTH, H * P_SIZE), 0.25, 4.0, ((0, 4), (1, 16), (2, 4)))
    seq_b = centred(seeds[1], (PROMPTS, PROMPT_LENGTH, G * N), N ** -0.5, 0.5, ((0, 4), (1, 16), (2, 4)))
    seq_c = centred(seeds[2], (PROMPTS, PROMPT_LENGTH, G * N), N ** -0.5, 0.5, ((0, 4), (1, 16), (2, 4)))
    seq_decay = draw_seq_decay(jax.random.fold_in(seeds[10], 71), 0)
    row_prompt = set_ends(jax.random.randint(seeds[4], (ROWS,), 0, PROMPTS), jax.random.fold_in(seeds[4], 1), 0, PROMPTS - 1).astype(jnp.int32)
    cache_slot = draw_cache_slot(jax.random.fold_in(seeds[10], 71), 0)
    step_input = centred(seeds[6], (STEPS, ROWS, H * P_SIZE), 2.0, 8.0, ((1, 64), (2, 4)))
    step_b = centred(seeds[7], (STEPS, ROWS, G * N), N ** -0.5, 0.5, ((1, 64), (2, 4)))
    step_c = centred(seeds[8], (STEPS, ROWS, G * N), N ** -0.5, 0.5, ((1, 64), (2, 4)))
    step_decay = jnp.clip(0.5 + 0.5 * jax.random.uniform(seeds[9], (STEPS, ROWS, H), jnp.float32) ** block_scale(seeds[9], (STEPS, ROWS, H), ((1, 64), (2, 4)), -0.2, 0.2), 0.5, 1.0)
    return dict(seq_input=seq_input, seq_b=seq_b, seq_c=seq_c, seq_decay=seq_decay, row_prompt=row_prompt, cache_slot=cache_slot, step_input=step_input, step_b=step_b, step_c=step_c, step_decay=step_decay)


HIGH = lax.Precision.HIGHEST


def prefill_prompt(inputs, b_proj, c_proj, decay):
    per_group = H // G
    count = PROMPT_LENGTH // Q
    x_blocks = inputs.reshape(count, Q, G, per_group, P_SIZE)
    b_blocks = b_proj.reshape(count, Q, G, N)
    c_blocks = c_proj.reshape(count, Q, G, N)
    d_blocks = decay.reshape(H, count, Q).transpose(1, 0, 2)
    lower = jnp.tril(jnp.ones((Q, Q), dtype=bool))

    def block_step(state, fragments):
        x_block, b_block, c_block, d_block = fragments
        cumulative = jnp.cumsum(d_block, axis=-1).reshape(G, per_group, Q)
        x_float = x_block.astype(jnp.float32)
        b_float = b_block.astype(jnp.float32)
        c_float = c_block.astype(jnp.float32)
        scores = jnp.einsum('ign,jgn->gij', c_float, b_float, precision=HIGH)
        gaps = cumulative[:, :, :, None] - cumulative[:, :, None, :]
        weights = (scores[:, None] * jnp.exp(jnp.where(lower, gaps, -jnp.inf))).astype(jnp.bfloat16)
        weights = lax.optimization_barrier(weights).astype(jnp.float32)
        inner = jnp.einsum('ghij,jghp->ighp', weights, x_float, precision=HIGH)
        entering = lax.optimization_barrier(state.astype(jnp.bfloat16)).astype(jnp.float32)
        entering = entering.reshape(G, per_group, P_SIZE, N)
        carried = jnp.einsum('ign,ghpn->ighp', c_float, entering, precision=HIGH)
        carried = carried * jnp.exp(cumulative).transpose(2, 0, 1)[..., None]
        output = (inner + carried).astype(jnp.bfloat16).reshape(Q, H * P_SIZE)
        last = cumulative[:, :, -1:]
        scaled = (jnp.exp(last - cumulative).transpose(2, 0, 1)[..., None] * x_float).astype(jnp.bfloat16)
        scaled = lax.optimization_barrier(scaled).astype(jnp.float32)
        term = jnp.einsum('jghp,jgn->ghpn', scaled, b_float, precision=HIGH).reshape(H, P_SIZE, N)
        state = jnp.exp(last.reshape(H))[:, None, None] * state + term
        return state, output

    final, outputs = lax.scan(block_step, jnp.zeros((H, P_SIZE, N), jnp.float32), (x_blocks, b_blocks, c_blocks, d_blocks))
    return outputs.reshape(PROMPT_LENGTH, H * P_SIZE), final


def reference(seq_input, seq_b, seq_c, seq_decay, row_prompt, cache_slot, step_input, step_b, step_c, step_decay):
    seq_output, finals = lax.map(lambda fragments: prefill_prompt(*fragments), (seq_input, seq_b, seq_c, seq_decay))
    per_group = H // G

    def decode_row(fragments):
        prompt, x_row, b_row, c_row, d_row = fragments
        state = lax.dynamic_index_in_dim(finals, prompt, 0, keepdims=False).reshape(G, per_group, P_SIZE, N)
        answers = []
        for step in range(STEPS):
            x_heads = x_row[step].astype(jnp.float32).reshape(G, per_group, P_SIZE)
            b_group = b_row[step].astype(jnp.float32).reshape(G, N)
            c_group = c_row[step].astype(jnp.float32).reshape(G, N)
            keep = d_row[step].reshape(G, per_group)
            state = keep[..., None, None] * state + x_heads[..., None] * b_group[:, None, None, :]
            answers.append(jnp.einsum('ghpn,gn->ghp', state, c_group, precision=HIGH).reshape(H * P_SIZE))
        return jnp.stack(answers).astype(jnp.bfloat16), state.astype(jnp.bfloat16).reshape(H, P_SIZE, N)

    row_answers, row_states = lax.map(decode_row, (row_prompt, step_input.transpose(1, 0, 2), step_b.transpose(1, 0, 2), step_c.transpose(1, 0, 2), step_decay.transpose(1, 0, 2)))
    step_output = row_answers.transpose(1, 0, 2)
    row_ids = jnp.arange(ROWS, dtype=jnp.int32)
    target = (row_ids // R_DEV) * R_DEV + cache_slot.astype(jnp.int32)
    state_cache = jnp.zeros((ROWS, H, P_SIZE, N), jnp.bfloat16).at[target].set(row_states)
    return seq_output, step_output, state_cache
```

```python
import functools
import math

import jax
import jax.numpy as jnp
import numpy as np
from jax import lax
from jax.experimental import pallas as pl
from jax.experimental.pallas import tpu as pltpu
from jax.sharding import PartitionSpec as P

MESH = pl.DeviceIdType.MESH
P_SIZE = 64
N = 128
B = 128
STEPS = 8
LOG2E = math.log2(math.e)
HIGH = lax.Precision.HIGHEST
F32 = jnp.float32
BF16 = jnp.bfloat16
CH = 4
MIB = 2**20


def dot(a, b, dims=((1,), (0,)), precision=None):
    return lax.dot_general(
        a, b, (dims, ((), ())), preferred_element_type=F32, precision=precision
    )


def spread_matrix(heads):
    row = np.arange(2 * heads)[:, None] % heads
    col = np.arange(heads * P_SIZE)[None, :] // P_SIZE
    return jnp.asarray((row == col).astype(np.float32), BF16)


def split_spread(v, spread):
    half = v.shape[1] // 2
    hi = v.astype(BF16)
    low = (v - hi.astype(F32)).astype(BF16)
    lane = lax.broadcasted_iota(jnp.int32, v.shape, 1)
    return dot(jnp.where(lane < half, hi, low), spread)


def block_sums(dec):
    dec2 = jnp.concatenate([dec, dec], axis=0) * LOG2E
    row = lax.broadcasted_iota(jnp.int32, (B, B), 0)
    col = lax.broadcasted_iota(jnp.int32, (B, B), 1)
    upper = (row <= col).astype(F32)
    cum = dot(dec2, upper, precision=HIGH)
    return cum, cum.T


def prep_kernel(x_ref, b_ref, c_ref, d_ref, spread_ref, y_ref, s_ref, state, total):
    k = pl.program_id(0)
    heads = d_ref.shape[0]
    groups = b_ref.shape[1] // N
    per = heads // groups
    wide = per * P_SIZE

    @pl.when(k == 0)
    def _():
        state[...] = jnp.zeros_like(state)
        total[...] = jnp.zeros_like(total)

    cum, cum_t = block_sums(d_ref[...])
    last = cum_t[B - 1 : B, :]
    spread = spread_ref[...]
    row = lax.broadcasted_iota(jnp.int32, (B, B), 0)
    col = lax.broadcasted_iota(jnp.int32, (B, B), 1)
    lane = lax.broadcasted_iota(jnp.int32, (B, 2 * P_SIZE), 1)
    for g in range(groups):
        lanes = pl.ds(g * wide, wide)
        spread_g = spread[:, g * wide : (g + 1) * wide]
        b = b_ref[:, g * N : (g + 1) * N]
        c = c_ref[:, g * N : (g + 1) * N]
        x = x_ref[:, lanes]
        before = state[:, lanes]
        grown = split_spread(jnp.exp2(cum_t), spread_g)
        carried = dot(c, before.astype(BF16)) * grown
        left = split_spread(jnp.exp2(last - cum_t), spread_g)
        scaled = (x.astype(F32) * left).astype(BF16)
        term = dot(b.T, scaled)
        keep = split_spread(jnp.broadcast_to(jnp.exp2(last), (8, 2 * heads)), spread_g)
        state[:, lanes] = before * keep[0:1, :] + term
        scores = jnp.where(row >= col, dot(c, b, ((1,), (1,))), 0.0)
        for pair in range(per // 2):
            weights = []
            for h in (g * per + 2 * pair, g * per + 2 * pair + 1):
                gap = jnp.minimum(cum_t[:, h : h + 1] - cum[h : h + 1, :], 0.0)
                weights.append((scores * jnp.exp2(gap)).astype(BF16))
            xp = x[:, pair * 2 * P_SIZE : (pair + 1) * 2 * P_SIZE]
            zero = jnp.zeros_like(xp)
            both = jnp.concatenate(
                [jnp.where(lane < P_SIZE, xp, zero), jnp.where(lane < P_SIZE, zero, xp)], axis=0
            )
            inner = dot(jnp.concatenate(weights, axis=1), both)
            at = pl.ds(g * wide + pair * 2 * P_SIZE, 2 * P_SIZE)
            y_ref[:, at] = (
                inner + carried[:, pair * 2 * P_SIZE : (pair + 1) * 2 * P_SIZE]
            ).astype(y_ref.dtype)
    total[...] += jnp.broadcast_to(last, total.shape)

    @pl.when(k == pl.num_programs(0) - 1)
    def _():
        keep = split_spread(jnp.exp2(total[...]), spread)
        for pair in range(heads // 2):
            at = pl.ds(pair * 2 * P_SIZE, 2 * P_SIZE)
            s_ref[pair, 0:N, :] = state[:, at]
            s_ref[pair, N : N + 8, :] = keep[:, pair * 2 * P_SIZE : (pair + 1) * 2 * P_SIZE]


def close_kernel(y_ref, c_ref, d_ref, e_ref, spread_ref, out_ref, enter, total):
    k = pl.program_id(0)
    groups = c_ref.shape[1] // N
    wide = y_ref.shape[1] // groups

    @pl.when(k == 0)
    def _():
        total[...] = jnp.zeros_like(total)
        for pair in range(e_ref.shape[0]):
            enter[:, pair * 2 * P_SIZE : (pair + 1) * 2 * P_SIZE] = e_ref[pair].astype(BF16)

    _, cum_t = block_sums(d_ref[...])
    grown = jnp.exp2(cum_t + total[0:1, :])
    for g in range(groups):
        lanes = pl.ds(g * wide, wide)
        carried = dot(c_ref[:, g * N : (g + 1) * N], enter[:, lanes])
        factor = split_spread(grown, spread_ref[:, g * wide : (g + 1) * wide])
        out_ref[:, lanes] = (y_ref[:, lanes].astype(F32) + carried * factor).astype(BF16)
    total[...] += jnp.broadcast_to(cum_t[B - 1 : B, :], total.shape)


def scan_kernel(
    sizes,
    s_ref,
    e_ref,
    g_ref,
    got,
    tops,
    staged,
    turned,
    z_send,
    z_recv,
    y_send,
    y_recv,
    e_send,
    e_recv,
    swap_send,
    swap_recv,
    fz_send,
    fz_recv,
    fl_send,
    fl_recv,
    fy_send,
    fy_recv,
    fc_send,
    fc_recv,
):
    nz, ny = sizes
    s, t, d = lax.axis_index("seq"), lax.axis_index("tp"), lax.axis_index("dp")
    y, z = s // nz, s % nz
    zl, core = d // 2, d % 2
    away = t != d

    def z_dev(i):
        return (y * nz + (z + i) % nz, t, d)

    def y_dev(i):
        return (((y + i) % ny) * nz + z, t, d)

    swap_dev = (s, d, t)
    zl_dev = (s, t, (1 - zl) * 2 + core)
    core_dev = (s, t, zl * 2 + 1 - core)

    barrier = pltpu.get_barrier_semaphore()
    others = [z_dev(i) for i in range(1, nz)] + [y_dev(i) for i in range(1, ny)]
    others += [zl_dev, core_dev]
    for dev in others:
        pl.semaphore_signal(barrier, inc=1, device_id=dev, device_id_type=MESH)

    @pl.when(away)
    def _():
        pl.semaphore_signal(barrier, inc=1, device_id=swap_dev, device_id_type=MESH)

    pl.semaphore_wait(barrier, jnp.where(away, len(others) + 1, len(others)))

    def copy(src, dst, send, recv, dev):
        return pltpu.make_async_remote_copy(
            src_ref=src, dst_ref=dst, send_sem=send, recv_sem=recv, device_id=dev,
            device_id_type=MESH,
        )

    def z_copy(c, i):
        return copy(
            s_ref.at[CH * ((z + i) % nz) + c], got.at[z, c], z_send.at[c, i - 1],
            z_recv.at[c, i - 1], z_dev(i),
        )

    def y_copy(c, i):
        return copy(
            tops.at[y, c], tops.at[y, c], y_send.at[c, i - 1], y_recv.at[c, i - 1], y_dev(i)
        )

    def e_copy(c, i):
        return copy(
            staged.at[(z + i) % nz, c], e_ref.at[CH * z + c], e_send.at[c, i - 1],
            e_recv.at[c, i - 1], z_dev(i),
        )

    def swap_copy(c):
        return copy(
            turned.at[c, pl.ds(32 * y, 32)], g_ref.at[c, y, t % 2, t // 2, z], swap_send.at[c],
            swap_recv.at[c], swap_dev,
        )

    def fz_copy(c, i):
        ref = g_ref.at[c, y, core, zl, z]
        return copy(ref, ref, fz_send.at[c, i - 1], fz_recv.at[c, i - 1], z_dev(i))

    def fl_copy(c):
        ref = g_ref.at[c, y, core, zl]
        return copy(ref, ref, fl_send.at[c], fl_recv.at[c], zl_dev)

    def fy_copy(c, i):
        ref = g_ref.at[c, y, core]
        return copy(ref, ref, fy_send.at[c, i - 1], fy_recv.at[c, i - 1], y_dev(i))

    def fc_copy(c, i):
        ref = g_ref.at[c, (y + ny - i) % ny, core]
        return copy(ref, ref, fc_send.at[c, i], fc_recv.at[c, i], core_dev)

    for c in range(CH):
        for i in range(1, nz):
            z_copy(c, i).start()
    for c in range(CH):
        got[z, c] = s_ref[CH * z + c]

    def stage_a(c):
        for i in range(1, nz):
            z_copy(c, i).wait_recv()
        top = got[0, c, 0:N]
        keep = got[0, c, N : N + 8]
        for k in range(1, nz):
            a = got[k, c, N : N + 8]
            top = top * a[0:1] + got[k, c, 0:N]
            keep = keep * a
        tops[y, c, 0:N] = top
        tops[y, c, N : N + 8] = keep
        for i in range(1, ny):
            y_copy(c, i).start()

    def stage_b(c):
        for i in range(1, ny):
            y_copy(c, i).wait_recv()
        enter = jnp.zeros((N, 2 * P_SIZE), F32)
        last = enter
        for k in range(ny):
            a = tops[k, c, N : N + 1]
            top = tops[k, c, 0:N]
            enter = jnp.where(k < y, enter * a + top, enter)
            last = last * a + top
        for k in range(nz):
            staged[k, c] = enter
            if k < nz - 1:
                enter = enter * got[k, c, N : N + 1] + got[k, c, 0:N]
        for i in range(1, nz):
            e_copy(c, i).start()
        e_ref[CH * z + c] = staged[z, c]
        turned[c] = last.T

        @pl.when(away)
        def _():
            swap_copy(c).start()

        @pl.when(jnp.logical_not(away))
        def _():
            g_ref[c, y, core, zl, z] = turned[c, pl.ds(32 * y, 32)]

    def stage_c(c):
        @pl.when(away)
        def _():
            swap_copy(c).wait_recv()

        for i in range(1, nz):
            fz_copy(c, i).start()

    def stage_d(c):
        for i in range(1, nz):
            fz_copy(c, i).wait_recv()
        fl_copy(c).start()

    def stage_e(c):
        fl_copy(c).wait_recv()
        for i in range(1, ny):
            fy_copy(c, i).start()
        fc_copy(c, 0).start()

    def stage_f(c):
        for i in range(1, ny):
            fy_copy(c, i).wait_recv()
            fc_copy(c, i).start()

    stages = (stage_a, stage_b, stage_c, stage_d, stage_e, stage_f)
    for step in range(CH + len(stages) - 1):
        for n, stage in enumerate(stages):
            if 0 <= step - n < CH:
                stage(step - n)

    for c in range(CH):
        for i in range(1, nz):
            e_copy(c, i).wait_recv()
            z_copy(c, i).wait_send()
            e_copy(c, i).wait_send()
            fz_copy(c, i).wait_send()
        for i in range(1, ny):
            y_copy(c, i).wait_send()
            fy_copy(c, i).wait_send()
        for i in range(ny):
            fc_copy(c, i).wait()
        fl_copy(c).wait_send()

        @pl.when(away)
        def _():
            swap_copy(c).wait_send()


def scan(s_ext, nz, ny):
    pairs = s_ext.shape[0]
    dma = pltpu.SemaphoreType.DMA
    vmem = pl.BlockSpec(memory_space=pltpu.VMEM)
    return pl.pallas_call(
        functools.partial(scan_kernel, (nz, ny)),
        out_shape=(
            jax.ShapeDtypeStruct((pairs, N, 2 * P_SIZE), F32),
            jax.ShapeDtypeStruct((CH, ny, 2, 2, nz, 32, N), F32),
        ),
        in_specs=[vmem],
        out_specs=(vmem, vmem),
        scratch_shapes=[
            pltpu.VMEM((nz, CH, N + 8, 2 * P_SIZE), F32),
            pltpu.VMEM((ny, CH, N + 8, 2 * P_SIZE), F32),
            pltpu.VMEM((nz, CH, N, 2 * P_SIZE), F32),
            pltpu.VMEM((CH, 2 * P_SIZE, N), F32),
            dma((CH, 3)), dma((CH, 3)),
            dma((CH, 3)), dma((CH, 3)),
            dma((CH, 3)), dma((CH, 3)),
            dma((CH,)), dma((CH,)),
            dma((CH, 3)), dma((CH, 3)),
            dma((CH,)), dma((CH,)),
            dma((CH, 3)), dma((CH, 3)),
            dma((CH, 4)), dma((CH, 4)),
        ],
        compiler_params=pltpu.CompilerParams(
            collective_id=0, has_side_effects=True, vmem_limit_bytes=24 * MIB
        ),
        name="scan",
    )(s_ext)


def decode_kernel(
    row_ref, slot_ref, g_ref, x_ref, b_ref, c_ref, d_ref, spread_ref, out_ref, cache_ref, coef
):
    chunk = pl.program_id(0)
    rows = x_ref.shape[1]
    heads = d_ref.shape[2]
    half = heads // 2
    spread = spread_ref[...]

    @pl.when(chunk == 0)
    def _():
        lane = lax.broadcasted_iota(jnp.int32, (STEPS * STEPS, heads), 1)
        for r in range(rows):
            keep = d_ref[:, r, :]
            b = b_ref[:, r, :].astype(F32)
            c = c_ref[:, r, :].astype(F32)
            grid = []
            for k in range(STEPS):
                line = [jnp.zeros((1, heads), F32)] * k + [jnp.ones((1, heads), F32)]
                for s in range(k + 1, STEPS):
                    line.append(line[-1] * keep[s : s + 1])
                grid.append(jnp.concatenate(line, axis=0))
            line = [keep[0:1]]
            for s in range(1, STEPS):
                line.append(line[-1] * keep[s : s + 1])
            reach = jnp.concatenate(grid, axis=0)
            meet = []
            for g in range(2):
                bg, cg = b[:, g * N : (g + 1) * N], c[:, g * N : (g + 1) * N]
                meet.append(
                    jnp.concatenate(
                        [jnp.sum(cg * bg[k : k + 1], axis=1, keepdims=True) for k in range(STEPS)],
                        axis=0,
                    )
                )
            met = reach * jnp.where(lane < half, meet[0], meet[1])
            tail = [grid[k][STEPS - 1 : STEPS] for k in range(STEPS)]
            table = jnp.concatenate([met] + line + tail, axis=0)
            coef[r] = jnp.concatenate([table, table], axis=1)

    for zi in range(4):
        g = zi // 2
        at = pl.ds(pl.multiple_of((4 * zi + chunk) * 2 * P_SIZE, 2 * P_SIZE), 2 * P_SIZE)
        sp = spread_ref[:, at]
        for r in range(rows):
            prompt = row_ref[r]
            f = g_ref[0, :, prompt % 2, prompt // 2, zi].reshape(2 * P_SIZE, N)
            b = b_ref[:, r, g * N : (g + 1) * N]
            c = c_ref[:, r, g * N : (g + 1) * N]
            x = x_ref[:, r, at].astype(F32)
            co = split_spread(coef[r], sp)
            f_hi = f.astype(BF16)
            f_low = (f - f_hi.astype(F32)).astype(BF16)
            seen = dot(c, f_hi, ((1,), (1,))) + dot(c, f_low, ((1,), (1,)))
            base = STEPS * STEPS
            answer = seen * co[base : base + STEPS]
            for k in range(STEPS):
                answer += co[k * STEPS : (k + 1) * STEPS] * x[k : k + 1]
            out_ref[:, r, at] = answer.astype(BF16)
            push = x * co[base + STEPS : base + 2 * STEPS]
            p_hi = push.astype(BF16).astype(F32)
            both = jnp.concatenate([p_hi, push - p_hi], axis=0)
            bb = jnp.concatenate([b, b], axis=0).astype(F32)
            gain = dot(both.T.astype(BF16), bb.astype(BF16))
            kept = jnp.broadcast_to(co[base + STEPS - 1 : base + STEPS], (2 * P_SIZE, N)).T
            cache_ref[slot_ref[r], zi, 0] = (f * kept + gain).astype(BF16)


def decode(row_prompt, cache_slot, g, x, b, c, keep, spread):
    rows = x.shape[1]
    heads = keep.shape[2]
    nz = g.shape[4]
    smem = pl.BlockSpec(memory_space=pltpu.SMEM)

    def whole(a):
        return pl.BlockSpec(a.shape, lambda i: (0,) * a.ndim)

    out, cache = pl.pallas_call(
        decode_kernel,
        grid=(CH,),
        out_shape=(
            jax.ShapeDtypeStruct(x.shape, BF16),
            jax.ShapeDtypeStruct((rows, nz, CH, 2 * P_SIZE, N), BF16),
        ),
        in_specs=[
            smem,
            smem,
            pl.BlockSpec((1,) + g.shape[1:], lambda i: (i, 0, 0, 0, 0, 0, 0)),
            whole(x),
            whole(b),
            whole(c),
            whole(keep),
            whole(spread),
        ],
        out_specs=(
            whole(x),
            pl.BlockSpec((rows, nz, 1, 2 * P_SIZE, N), lambda i: (0, 0, i, 0, 0)),
        ),
        scratch_shapes=[pltpu.VMEM((rows, STEPS * STEPS + 2 * STEPS, 2 * heads), F32)],
        compiler_params=pltpu.CompilerParams(
            dimension_semantics=("arbitrary",), vmem_limit_bytes=24 * MIB
        ),
        name="decode",
    )(row_prompt, cache_slot, g, x, b, c, keep, spread)
    return out, cache.reshape(rows, heads, P_SIZE, N)


def per_device(x, b, c, decay, row_prompt, cache_slot, step_x, step_b, step_c, step_decay):
    x, b, c, decay = x[0], b[0], c[0], decay[0]
    length, wide = x.shape
    heads = decay.shape[0]
    pairs = heads // 2
    spread = spread_matrix(heads)
    nz, ny = 4, lax.axis_size("seq") // 4

    def rows(a):
        return pl.BlockSpec((B, a.shape[1]), lambda i: (i, 0))

    def whole(a):
        return pl.BlockSpec(a.shape, lambda i: (0,) * a.ndim)

    lanes = pl.BlockSpec((heads, B), lambda i: (0, i))
    params = pltpu.CompilerParams(
        dimension_semantics=("arbitrary",), vmem_limit_bytes=32 * MIB
    )
    part, s_ext = pl.pallas_call(
        prep_kernel,
        grid=(length // B,),
        out_shape=(
            jax.ShapeDtypeStruct(x.shape, BF16),
            jax.ShapeDtypeStruct((pairs, N + 8, 2 * P_SIZE), F32),
        ),
        in_specs=[rows(x), rows(b), rows(c), lanes, whole(spread)],
        out_specs=(rows(x), pl.BlockSpec((pairs, N + 8, 2 * P_SIZE), lambda i: (0, 0, 0))),
        scratch_shapes=[pltpu.VMEM((N, wide), F32), pltpu.VMEM((8, 2 * heads), F32)],
        compiler_params=params,
        name="prep",
    )(x, b, c, decay, spread)
    enter, finals = scan(s_ext, nz, ny)
    seq_output = pl.pallas_call(
        close_kernel,
        grid=(length // B,),
        out_shape=jax.ShapeDtypeStruct(x.shape, BF16),
        in_specs=[rows(x), rows(c), lanes, whole(enter), whole(spread)],
        out_specs=rows(x),
        scratch_shapes=[pltpu.VMEM((N, wide), BF16), pltpu.VMEM((8, 2 * heads), F32)],
        compiler_params=params,
        name="close",
    )(part, c, decay, enter, spread)
    step_output, state_cache = decode(
        row_prompt, cache_slot, finals, step_x, step_b, step_c, step_decay, spread
    )
    return seq_output[None], step_output, state_cache


def solution(mesh):
    return jax.shard_map(
        per_device,
        mesh=mesh,
        in_specs=(
            P("tp", "seq", "dp"),
            P("tp", "seq", "dp"),
            P("tp", "seq", "dp"),
            P("tp", "dp", "seq"),
            P(("seq", "dp")),
            P(("seq", "dp")),
            P(None, ("seq", "dp"), "tp"),
            P(None, ("seq", "dp"), "tp"),
            P(None, ("seq", "dp"), "tp"),
            P(None, ("seq", "dp"), "tp"),
        ),
        out_specs=(
            P("tp", "seq", "dp"),
            P(None, ("seq", "dp"), "tp"),
            P(("seq", "dp"), "tp", None, None),
        ),
        check_vma=False,
    )
```

```python
import functools
import math

import jax
import jax.numpy as jnp
from jax import lax
from jax.experimental import pallas as pl
from jax.experimental.pallas import tpu as pltpu
from jax.sharding import PartitionSpec as P

MESH = pl.DeviceIdType.MESH
P_SIZE = 64
N = 128
B = 128
STEPS = 8
LOG2E = math.log2(math.e)
HIGH = lax.Precision.HIGHEST
F32 = jnp.float32
BF16 = jnp.bfloat16
CH = 4
MIB = 2**20


def dot(a, b, dims=((1,), (0,)), precision=None):
    return lax.dot_general(
        a, b, (dims, ((), ())), preferred_element_type=F32, precision=precision
    )


def spread_matrix(shape):
    heads = shape[0] // 2
    row = lax.broadcasted_iota(jnp.int32, shape, 0)
    lane = lax.broadcasted_iota(jnp.int32, shape, 1)
    return (row % heads == lane // P_SIZE).astype(F32).astype(BF16)


def pair_lanes(pair):
    return pl.ds(pl.multiple_of(pair * 2 * P_SIZE, 2 * P_SIZE), 2 * P_SIZE)


def hi_low(v):
    hi = v.astype(BF16)
    lane = lax.broadcasted_iota(jnp.int32, v.shape, 1)
    return jnp.where(lane < v.shape[1] // 2, hi, (v - hi.astype(F32)).astype(BF16))


def decode_tables(x_ref, b_ref, c_ref, d_ref, spread_ref, pre_ref, reach_ref, push_ref, last_ref, cc_ref, bb_ref):
    rows, heads = d_ref.shape[1], d_ref.shape[2]
    lane = lax.broadcasted_iota(jnp.int32, (STEPS * STEPS, heads), 1)
    x_all = x_ref[...].astype(F32)
    b_all = b_ref[...].astype(F32)
    c_all = c_ref[...].astype(F32)
    pushes, cs, bs = [], [], []
    for r in range(rows):
        keep = d_ref[:, r, :]
        x, b, c = x_all[:, r, :], b_all[:, r, :], c_all[:, r, :]
        grid = []
        for k in range(STEPS):
            line = [jnp.zeros((1, heads), F32)] * k + [jnp.ones((1, heads), F32)]
            for s in range(k + 1, STEPS):
                line.append(line[-1] * keep[s : s + 1])
            grid.append(jnp.concatenate(line, axis=0))
        line = [keep[0:1]]
        for s in range(1, STEPS):
            line.append(line[-1] * keep[s : s + 1])
        meet = []
        for g in range(2):
            bg, cg = b[:, g * N : (g + 1) * N], c[:, g * N : (g + 1) * N]
            meet.append(
                jnp.concatenate(
                    [jnp.sum(cg * bg[k : k + 1], axis=1, keepdims=True) for k in range(STEPS)],
                    axis=0,
                )
            )
        met = jnp.concatenate(grid, axis=0) * jnp.where(lane < heads // 2, meet[0], meet[1])
        left = [grid[k][STEPS - 1 : STEPS] for k in range(STEPS)]
        table = jnp.concatenate([met] + line + left, axis=0)
        co = dot(hi_low(jnp.concatenate([table, table], axis=1)), spread_ref[...])
        base = STEPS * STEPS
        local = co[0:STEPS] * x[0:1]
        for k in range(1, STEPS):
            local += co[k * STEPS : (k + 1) * STEPS] * x[k : k + 1]
        pre_ref[r] = local
        reach_ref[r] = co[base : base + STEPS]
        push = x * co[base + STEPS : base + 2 * STEPS]
        hi = push.astype(BF16).astype(F32)
        pushes += [hi, push - hi]
        last_ref[r] = jnp.broadcast_to(line[-1], (N, heads)).T
        cs.append(c)
        bs.append(b)
    pushes = jnp.concatenate(pushes, axis=0)
    for pair in range(heads // 2):
        at = pl.ds(pair * 2 * P_SIZE, 2 * P_SIZE)
        push_ref[at, :] = pushes[:, pair * 2 * P_SIZE : (pair + 1) * 2 * P_SIZE].T.astype(BF16)
    cs = jnp.concatenate(cs, axis=0).astype(BF16)
    for g in range(2):
        cg = cs[:, g * N : (g + 1) * N]
        cc_ref[g] = jnp.concatenate([cg, cg], axis=1)
        lines = []
        for r in range(rows):
            b = bs[r][:, g * N : (g + 1) * N]
            zero = jnp.zeros((2 * STEPS, N), F32)
            mine = jnp.concatenate([b, b], axis=0)
            lines.append(
                jnp.concatenate([mine if q == r else zero for q in range(rows)], axis=1)
            )
        bb_ref[g] = jnp.concatenate(lines, axis=0).astype(BF16)


def core_kernel(
    sizes,
    x_hbm,
    b_hbm,
    c_hbm,
    d_hbm,
    sx_hbm,
    sb_hbm,
    sc_hbm,
    sd_hbm,
    out_hbm,
    g_hbm,
    pre_hbm,
    reach_hbm,
    push_hbm,
    last_hbm,
    cc_hbm,
    bb_hbm,
    xv,
    bv,
    cv,
    dv,
    sx_ref,
    sb_ref,
    sc_ref,
    sd_ref,
    out_ref,
    g_ref,
    pre_ref,
    reach_ref,
    push_ref,
    last_ref,
    cc_ref,
    bb_ref,
    spread_ref,
    bt,
    part,
    state,
    cum,
    cum_t,
    grown,
    remain,
    s_ref,
    e_ref,
    got,
    tops,
    staged,
    turned,
    x_sem,
    in_sem,
    out_sem,
    g_sem,
    table_sem,
    z_send,
    z_recv,
    y_send,
    y_recv,
    e_send,
    e_recv,
    fz_send,
    fz_recv,
    fl_send,
    fl_recv,
    fy_send,
    fy_recv,
    fc_send,
    fc_recv,
):
    nz, ny = sizes
    length, wide = xv.shape
    heads = dv.shape[0]
    groups = bv.shape[1] // N
    per = heads // groups
    blocks = length // B
    s, t, d = lax.axis_index("seq"), lax.axis_index("tp"), lax.axis_index("dp")
    y, z = s // nz, s % nz
    zl, core = d // 2, d % 2
    away = t != d

    def x_load(pair):
        at = pair_lanes(pair)
        return pltpu.make_async_copy(x_hbm.at[:, at], xv.at[:, at], x_sem.at[pair])

    loads = [
        pltpu.make_async_copy(src, dst, in_sem.at[n])
        for n, (src, dst) in enumerate(
            (
                (d_hbm, dv), (b_hbm, bv), (c_hbm, cv), (sx_hbm, sx_ref), (sb_hbm, sb_ref),
                (sc_hbm, sc_ref), (sd_hbm, sd_ref),
            )
        )
    ]
    tables = [
        pltpu.make_async_copy(src, dst, table_sem.at[n])
        for n, (src, dst) in enumerate(
            (
                (pre_ref, pre_hbm), (reach_ref, reach_hbm), (push_ref, push_hbm),
                (last_ref, last_hbm), (cc_ref, cc_hbm), (bb_ref, bb_hbm),
            )
        )
    ]

    def y_store(pair):
        at = pair_lanes(pair)
        return pltpu.make_async_copy(out_ref.at[:, at], out_hbm.at[:, at], out_sem.at[pair])

    def g_store(c):
        return pltpu.make_async_copy(g_ref.at[c], g_hbm.at[c], g_sem.at[c])

    loads[0].start()
    loads[1].start()
    for c in range(CH):
        for q in range(nz):
            x_load(CH * q + c).start()
    for load in loads[2:]:
        load.start()
    spread_ref[...] = spread_matrix(spread_ref.shape)

    def z_dev(i):
        return (y * nz + (z + i) % nz, t, d)

    def y_dev(i):
        return (((y + i) % ny) * nz + z, t, d)

    def cross_dev(i):
        return (y * nz + (z + i) % nz, d, t)

    zl_dev = (s, t, (1 - zl) * 2 + core)
    core_dev = (s, t, zl * 2 + 1 - core)

    barrier = pltpu.get_barrier_semaphore()
    others = [z_dev(i) for i in range(1, nz)] + [y_dev(i) for i in range(1, ny)]
    others += [zl_dev, core_dev]
    for dev in others:
        pl.semaphore_signal(barrier, inc=1, device_id=dev, device_id_type=MESH)

    @pl.when(away)
    def _():
        for i in range(nz):
            pl.semaphore_signal(barrier, inc=1, device_id=cross_dev(i), device_id_type=MESH)

    pl.semaphore_wait(barrier, jnp.where(away, len(others) + nz, len(others)))

    def copy(src, dst, send, recv, dev):
        return pltpu.make_async_remote_copy(
            src_ref=src, dst_ref=dst, send_sem=send, recv_sem=recv, device_id=dev,
            device_id_type=MESH,
        )

    def z_copy(c, i):
        return copy(
            s_ref.at[CH * ((z + i) % nz) + c], got.at[z, c], z_send.at[c, i - 1],
            z_recv.at[c, i - 1], z_dev(i),
        )

    def y_copy(c, i):
        return copy(
            tops.at[y, c], tops.at[y, c], y_send.at[c, i - 1], y_recv.at[c, i - 1], y_dev(i)
        )

    def e_copy(c, i):
        return copy(
            staged.at[(z + i) % nz, c], e_ref.at[CH * z + c], e_send.at[c, i - 1],
            e_recv.at[c, i - 1], z_dev(i),
        )

    def fz_copy(c, i):
        return copy(
            turned.at[c, pl.ds(32 * y, 32)], g_ref.at[c, y, t % 2, t // 2, z], fz_send.at[c, i],
            fz_recv.at[c, i], cross_dev(i),
        )

    def fl_copy(c):
        ref = g_ref.at[c, y, core, zl]
        return copy(ref, ref, fl_send.at[c], fl_recv.at[c], zl_dev)

    def fy_copy(c, i, other):
        ref = g_ref.at[c, y, core, 1 - zl if other else zl]
        n = 3 * other + i - 1
        return copy(ref, ref, fy_send.at[c, n], fy_recv.at[c, n], y_dev(i))

    def fc_copy(c, i):
        ref = g_ref.at[c, (y + ny - i) % ny, core]
        return copy(ref, ref, fc_send.at[c, i], fc_recv.at[c, i], core_dev)

    loads[0].wait()
    row = lax.broadcasted_iota(jnp.int32, (B, B), 0)
    col = lax.broadcasted_iota(jnp.int32, (B, B), 1)
    upper = (row <= col).astype(F32)
    lead = jnp.zeros((1, 2 * heads), F32)
    leads = []
    for k in range(blocks):
        at = pl.ds(k * B, B)
        dec = dv[:, at]
        sums = dot(jnp.concatenate([dec, dec], axis=0) * LOG2E, upper, precision=HIGH)
        cum[:, at] = sums
        cum_t[at, :] = sums.T
        leads.append(lead)
        lead = lead + cum_t[k * B + B - 1 : k * B + B, :]
    for k in range(blocks):
        at = pl.ds(k * B, B)
        whole = cum_t[at, :] + leads[k]
        grown[at, :] = hi_low(jnp.exp2(whole))
        remain[at, :] = hi_low(jnp.exp2(jnp.minimum(lead - whole, 0.0)))
    keep = hi_low(jnp.broadcast_to(jnp.exp2(lead), (16, 2 * heads)))

    loads[1].wait()
    for k in range(blocks):
        for g in range(groups):
            at = pl.ds(k * B, B)
            bt[g, :, at] = bv[at, g * N : (g + 1) * N].T

    def own_state(c, carry):
        left = remain[...]
        for q in range(nz):
            pair = CH * q + c
            g = q * CH * 2 // per
            x_load(pair).wait()
            at = pair_lanes(pair)
            sp = spread_ref[:, at]
            scaled = (xv[:, at].astype(F32) * dot(left, sp)).astype(BF16)
            s_ref[pair, 0:N] = dot(bt[g], scaled)
            s_ref[pair, N : N + 8] = dot(keep, sp)[0:8]
        for i in range(1, nz):
            z_copy(c, i).start()
        got[z, c] = s_ref[CH * z + c]
        return carry

    with jax.named_scope("own_state"):
        lax.fori_loop(0, CH, own_state, 0)
    for load in loads[2:]:
        load.wait()
    with jax.named_scope("decode_tables"):
        decode_tables(
            sx_ref, sb_ref, sc_ref, sd_ref, spread_ref, pre_ref, reach_ref, push_ref, last_ref,
            cc_ref, bb_ref,
        )
    for table in tables:
        table.start()
    state[...] = jnp.zeros((N, wide), F32)
    lane = lax.broadcasted_iota(jnp.int32, (B, 2 * P_SIZE), 1)

    def block(k):
        rows = pl.ds(pl.multiple_of(k * B, B), B)
        sums, sums_t = cum[:, rows], cum_t[rows, :]
        last = sums_t[B - 1 : B, :]
        grow = hi_low(jnp.exp2(sums_t))
        left = hi_low(jnp.exp2(last - sums_t))
        fade = hi_low(jnp.broadcast_to(jnp.exp2(last), (16, 2 * heads)))
        for g in range(groups):
            lanes = pl.ds(g * per * P_SIZE, per * P_SIZE)
            sp = spread_ref[:, lanes]
            c = cv[rows, g * N : (g + 1) * N]
            x = xv[rows, lanes]
            before = state[:, lanes]
            carried = dot(c, before.astype(BF16)) * dot(grow, sp)
            scaled = (x.astype(F32) * dot(left, sp)).astype(BF16)
            term = dot(bt[g, :, rows], scaled)
            state[:, lanes] = before * dot(fade, sp)[0:1, :] + term
            scores = jnp.where(row >= col, dot(c, bt[g, :, rows]), 0.0)
            for n in range(per // 2):
                weights = []
                for h in (g * per + 2 * n, g * per + 2 * n + 1):
                    gap = jnp.minimum(sums_t[:, h : h + 1] - sums[h : h + 1, :], 0.0)
                    weights.append((scores * jnp.exp2(gap)).astype(BF16))
                here = slice(n * 2 * P_SIZE, (n + 1) * 2 * P_SIZE)
                zero = jnp.zeros((B, 2 * P_SIZE), BF16)
                both = jnp.concatenate(
                    [
                        jnp.where(lane < P_SIZE, x[:, here], zero),
                        jnp.where(lane < P_SIZE, zero, x[:, here]),
                    ],
                    axis=0,
                )
                inner = dot(jnp.concatenate(weights, axis=1), both)
                part[rows, pl.ds((g * per + 2 * n) * P_SIZE, 2 * P_SIZE)] = inner + carried[:, here]

    def stage_a(c):
        for i in range(1, nz):
            z_copy(c, i).wait_recv()
        top = got[0, c, 0:N]
        kept = got[0, c, N : N + 8]
        for k in range(1, nz):
            a = got[k, c, N : N + 8]
            top = top * a[0:1] + got[k, c, 0:N]
            kept = kept * a
        tops[y, c, 0:N] = top
        tops[y, c, N : N + 8] = kept
        for i in range(1, ny):
            y_copy(c, i).start()

    def stage_b(c):
        for i in range(1, ny):
            y_copy(c, i).wait_recv()
        enter = jnp.zeros((N, 2 * P_SIZE), F32)
        last = enter
        for k in range(ny):
            a = tops[k, c, N : N + 1]
            top = tops[k, c, 0:N]
            enter = jnp.where(k < y, enter * a + top, enter)
            last = last * a + top
        turned[c] = last.T

        @pl.when(away)
        def _():
            fz_copy(c, 0).start()

        @pl.when(jnp.logical_not(away))
        def _():
            g_ref[c, y, core, zl, z] = turned[c, pl.ds(32 * y, 32)]

        for i in range(1, nz):
            fz_copy(c, i).start()
        for k in range(nz):
            staged[k, c] = enter
            if k < nz - 1:
                enter = enter * got[k, c, N : N + 1] + got[k, c, 0:N]
        e_ref[CH * z + c] = staged[z, c]
        for i in range(1, nz):
            e_copy(c, i).start()

    def stage_c(c):
        @pl.when(away)
        def _():
            fz_copy(c, 0).wait_recv()

        for i in range(1, nz):
            fz_copy(c, i).wait_recv()
        fl_copy(c).start()
        for i in range(1, ny):
            fy_copy(c, i, 0).start()

    def stage_d(c):
        fl_copy(c).wait_recv()
        for i in range(1, ny):
            fy_copy(c, i, 1).start()
        fc_copy(c, 0).start()

    def stage_e(c):
        for i in range(1, ny):
            fy_copy(c, i, 0).wait_recv()
            fy_copy(c, i, 1).wait_recv()
            fc_copy(c, i).start()

    def stage_f(c):
        for i in range(ny):
            fc_copy(c, i).wait_recv()
        g_store(c).start()

    def close(c):
        for i in range(1, nz):
            e_copy(c, i).wait_recv()
        for q in range(nz):
            pair = CH * q + c
            g = q * CH * 2 // per
            at = pair_lanes(pair)
            carried = dot(cv[:, g * N : (g + 1) * N], e_ref[pair].astype(BF16))
            carried = carried * dot(grown[...], spread_ref[:, at])
            out_ref[:, at] = (part[:, at] + carried).astype(BF16)
            y_store(pair).start()

    stages = (
        (stage_a, 0), (stage_b, 1), (stage_c, 2), (stage_d, 3), (stage_e, 4), (stage_f, 5),
        (close, CLOSE),
    )
    for k in range(EARLY):
        block(k)

    def step(n, carry):
        for stage, after in stages:

            @pl.when(jnp.logical_and(n >= after, n < after + CH))
            def _():
                with jax.named_scope(stage.__name__):
                    stage(n - after)

        @pl.when(n < blocks - EARLY)
        def _():
            with jax.named_scope("block"):
                block(n + EARLY)

        return carry

    lax.fori_loop(0, CLOSE + CH, step, 0)

    def drain(c, carry):
        for i in range(1, nz):
            z_copy(c, i).wait_send()
            e_copy(c, i).wait_send()
            fz_copy(c, i).wait_send()
        for i in range(1, ny):
            y_copy(c, i).wait_send()
            fy_copy(c, i, 0).wait_send()
            fy_copy(c, i, 1).wait_send()
        for i in range(ny):
            fc_copy(c, i).wait_send()
        g_store(c).wait()
        for q in range(nz):
            y_store(CH * q + c).wait()
        fl_copy(c).wait_send()

        @pl.when(away)
        def _():
            fz_copy(c, 0).wait_send()

        return carry

    with jax.named_scope("drain"):
        lax.fori_loop(0, CH, drain, 0)
        for table in tables:
            table.wait()


CLOSE = 6
EARLY = 2


def core(x, b, c, decay, sx, sb, sc, sd, nz, ny):
    length, wide = x.shape
    heads = decay.shape[0]
    pairs = heads // 2
    rows = sx.shape[1]
    dma = pltpu.SemaphoreType.DMA
    hbm = pl.BlockSpec(memory_space=pl.ANY)
    pair_shape = (N, 2 * P_SIZE)
    outs = (
        jax.ShapeDtypeStruct(x.shape, BF16),
        jax.ShapeDtypeStruct((CH, ny, 2, 2, nz, 32, N), F32),
        jax.ShapeDtypeStruct((rows, STEPS, wide), F32),
        jax.ShapeDtypeStruct((rows, STEPS, wide), F32),
        jax.ShapeDtypeStruct((wide, 2 * STEPS * rows), BF16),
        jax.ShapeDtypeStruct((rows, heads, N), F32),
        jax.ShapeDtypeStruct((2, rows * STEPS, 2 * N), BF16),
        jax.ShapeDtypeStruct((2, 2 * STEPS * rows, rows * N), BF16),
    )
    return pl.pallas_call(
        functools.partial(core_kernel, (nz, ny)),
        out_shape=outs,
        in_specs=[hbm] * 8,
        out_specs=(hbm,) * len(outs),
        scratch_shapes=[
            pltpu.VMEM(x.shape, BF16),
            pltpu.VMEM(b.shape, BF16),
            pltpu.VMEM(c.shape, BF16),
            pltpu.VMEM(decay.shape, F32),
            pltpu.VMEM(sx.shape, BF16),
            pltpu.VMEM(sb.shape, BF16),
            pltpu.VMEM(sc.shape, BF16),
            pltpu.VMEM(sd.shape, F32),
        ]
        + [pltpu.VMEM(out.shape, out.dtype) for out in outs]
        + [
            pltpu.VMEM((2 * heads, wide), BF16),
            pltpu.VMEM((2, N, length), BF16),
            pltpu.VMEM(x.shape, F32),
            pltpu.VMEM((N, wide), F32),
            pltpu.VMEM((2 * heads, length), F32),
            pltpu.VMEM((length, 2 * heads), F32),
            pltpu.VMEM((length, 2 * heads), BF16),
            pltpu.VMEM((length, 2 * heads), BF16),
            pltpu.VMEM((pairs, N + 8, 2 * P_SIZE), F32),
            pltpu.VMEM((pairs,) + pair_shape, F32),
            pltpu.VMEM((nz, CH, N + 8, 2 * P_SIZE), F32),
            pltpu.VMEM((ny, CH, N + 8, 2 * P_SIZE), F32),
            pltpu.VMEM((nz, CH) + pair_shape, F32),
            pltpu.VMEM((CH, 2 * P_SIZE, N), F32),
            dma((pairs,)),
            dma((7,)),
            dma((pairs,)),
            dma((CH,)),
            dma((6,)),
            dma((CH, 3)), dma((CH, 3)),
            dma((CH, 3)), dma((CH, 3)),
            dma((CH, 3)), dma((CH, 3)),
            dma((CH, 4)), dma((CH, 4)),
            dma((CH,)), dma((CH,)),
            dma((CH, 6)), dma((CH, 6)),
            dma((CH, 4)), dma((CH, 4)),
        ],
        compiler_params=pltpu.CompilerParams(
            collective_id=0, has_side_effects=True, vmem_limit_bytes=60 * MIB
        ),
        name="core",
    )(x, b, c, decay, sx, sb, sc, sd)


def decode_kernel(
    row_ref, slot_ref, y_in, g_ref, pre_ref, reach_ref, push_ref, last_ref, cc_ref, bb_ref,
    y_out, out_ref, cache_ref,
):
    chunk = pl.program_id(0)
    rows = pre_ref.shape[0]
    y_out[...] = y_in[...]

    for zi in range(4):
        g = zi // 2
        pair = CH * zi + chunk
        at = pair_lanes(pair)
        seen = []
        for prompt in range(4):
            f = g_ref[0, :, prompt % 2, prompt // 2, zi].reshape(2 * P_SIZE, N)
            hi = f.astype(BF16)
            low = (f - hi.astype(F32)).astype(BF16)
            seen.append(dot(cc_ref[g], jnp.concatenate([hi, low], axis=1), ((1,), (1,))))
        gain = dot(push_ref[at, :], bb_ref[g])
        for r in range(rows):
            mine = row_ref[r]
            pick = seen[0][r * STEPS : (r + 1) * STEPS]
            for prompt in range(1, 4):
                pick = jnp.where(mine == prompt, seen[prompt][r * STEPS : (r + 1) * STEPS], pick)
            out_ref[:, r, at] = (pick * reach_ref[r, :, at] + pre_ref[r, :, at]).astype(BF16)
            f = g_ref[0, :, mine % 2, mine // 2, zi].reshape(2 * P_SIZE, N)
            kept = jnp.concatenate(
                [
                    jnp.broadcast_to(last_ref[r, pl.ds(2 * pair + n, 1), :], (P_SIZE, N))
                    for n in range(2)
                ],
                axis=0,
            )
            cache_ref[slot_ref[r], zi, 0] = (f * kept + gain[:, r * N : (r + 1) * N]).astype(BF16)


def decode(row_prompt, cache_slot, y, g, tables, shape):
    rows = shape[1]
    nz = g.shape[4]
    heads = shape[2] // P_SIZE
    smem = pl.BlockSpec(memory_space=pltpu.SMEM)
    part = pl.BlockSpec((y.shape[0] // CH, y.shape[1]), lambda i: (i, 0))

    def whole(s):
        return pl.BlockSpec(s, lambda i: (0,) * len(s))

    seq, out, cache = pl.pallas_call(
        decode_kernel,
        grid=(CH,),
        out_shape=(
            jax.ShapeDtypeStruct(y.shape, BF16),
            jax.ShapeDtypeStruct(shape, BF16),
            jax.ShapeDtypeStruct((rows, nz, CH, 2 * P_SIZE, N), BF16),
        ),
        in_specs=[
            smem,
            smem,
            part,
            pl.BlockSpec((1,) + g.shape[1:], lambda i: (i, 0, 0, 0, 0, 0, 0)),
        ]
        + [whole(a.shape) for a in tables],
        out_specs=(
            part,
            whole(shape),
            pl.BlockSpec((rows, nz, 1, 2 * P_SIZE, N), lambda i: (0, 0, i, 0, 0)),
        ),
        compiler_params=pltpu.CompilerParams(
            dimension_semantics=("arbitrary",), vmem_limit_bytes=60 * MIB
        ),
        name="decode",
    )(row_prompt, cache_slot, y, g, *tables)
    return seq, out, cache.reshape(rows, heads, P_SIZE, N)


def per_device(x, b, c, decay, row_prompt, cache_slot, step_x, step_b, step_c, step_decay):
    nz, ny = 4, lax.axis_size("seq") // 4
    y, g, *tables = core(
        x[0], b[0], c[0], decay[0], step_x, step_b, step_c, step_decay, nz, ny
    )
    seq, out, cache = decode(row_prompt, cache_slot, y, g, tables, step_x.shape)
    return seq[None], out, cache


def solution(mesh):
    return jax.shard_map(
        per_device,
        mesh=mesh,
        in_specs=(
            P("tp", "seq", "dp"),
            P("tp", "seq", "dp"),
            P("tp", "seq", "dp"),
            P("tp", "dp", "seq"),
            P(("seq", "dp")),
            P(("seq", "dp")),
            P(None, ("seq", "dp"), "tp"),
            P(None, ("seq", "dp"), "tp"),
            P(None, ("seq", "dp"), "tp"),
            P(None, ("seq", "dp"), "tp"),
        ),
        out_specs=(
            P("tp", "seq", "dp"),
            P(None, ("seq", "dp"), "tp"),
            P(("seq", "dp"), "tp", None, None),
        ),
        check_vma=False,
    )
```

```python
import functools
import math

import jax
import jax.numpy as jnp
from jax import lax
from jax.experimental import pallas as pl
from jax.experimental.pallas import tpu as pltpu
from jax.sharding import PartitionSpec as P

MESH = pl.DeviceIdType.MESH
P_SIZE = 64
N = 128
B = 128
STEPS = 8
LOG2E = math.log2(math.e)
F32 = jnp.float32
BF16 = jnp.bfloat16
CH = 4
MIB = 2**20


def dot(a, b, dims=((1,), (0,)), precision=None):
    return lax.dot_general(
        a, b, (dims, ((), ())), preferred_element_type=F32, precision=precision
    )


def spread_matrix(shape):
    heads = shape[0] // 2
    row = lax.broadcasted_iota(jnp.int32, shape, 0)
    lane = lax.broadcasted_iota(jnp.int32, shape, 1)
    return (row % heads == lane // P_SIZE).astype(F32).astype(BF16)


def pair_lanes(pair):
    return pl.ds(pl.multiple_of(pair * 2 * P_SIZE, 2 * P_SIZE), 2 * P_SIZE)


def hi_low(v):
    hi = v.astype(BF16)
    lane = lax.broadcasted_iota(jnp.int32, v.shape, 1)
    return jnp.where(lane < v.shape[1] // 2, hi, (v - hi.astype(F32)).astype(BF16))


def decode_tables(x_ref, b_ref, c_ref, d_ref, spread_ref, pre_ref, reach_ref, push_ref, last_ref, cc_ref, bb_ref):
    rows, heads = d_ref.shape[1], d_ref.shape[2]
    lane = lax.broadcasted_iota(jnp.int32, (STEPS * STEPS, heads), 1)
    x_all = x_ref[...].astype(F32)
    b_all = b_ref[...].astype(F32)
    c_all = c_ref[...].astype(F32)
    pushes, cs, bs = [], [], []
    for r in range(rows):
        keep = d_ref[:, r, :]
        x, b, c = x_all[:, r, :], b_all[:, r, :], c_all[:, r, :]
        grid = []
        for k in range(STEPS):
            line = [jnp.zeros((1, heads), F32)] * k + [jnp.ones((1, heads), F32)]
            for s in range(k + 1, STEPS):
                line.append(line[-1] * keep[s : s + 1])
            grid.append(jnp.concatenate(line, axis=0))
        line = [keep[0:1]]
        for s in range(1, STEPS):
            line.append(line[-1] * keep[s : s + 1])
        meet = []
        for g in range(2):
            bg, cg = b[:, g * N : (g + 1) * N], c[:, g * N : (g + 1) * N]
            meet.append(
                jnp.concatenate(
                    [jnp.sum(cg * bg[k : k + 1], axis=1, keepdims=True) for k in range(STEPS)],
                    axis=0,
                )
            )
        met = jnp.concatenate(grid, axis=0) * jnp.where(lane < heads // 2, meet[0], meet[1])
        left = [grid[k][STEPS - 1 : STEPS] for k in range(STEPS)]
        table = jnp.concatenate([met] + line + left, axis=0)
        co = dot(hi_low(jnp.concatenate([table, table], axis=1)), spread_ref[...])
        base = STEPS * STEPS
        local = co[0:STEPS] * x[0:1]
        for k in range(1, STEPS):
            local += co[k * STEPS : (k + 1) * STEPS] * x[k : k + 1]
        pre_ref[r] = local
        reach_ref[r] = co[base : base + STEPS]
        push = x * co[base + STEPS : base + 2 * STEPS]
        hi = push.astype(BF16).astype(F32)
        pushes += [hi, push - hi]
        last_ref[r] = jnp.broadcast_to(line[-1], (N, heads)).T
        cs.append(c)
        bs.append(b)
    pushes = jnp.concatenate(pushes, axis=0)
    for pair in range(heads // 2):
        at = pl.ds(pair * 2 * P_SIZE, 2 * P_SIZE)
        push_ref[at, :] = pushes[:, pair * 2 * P_SIZE : (pair + 1) * 2 * P_SIZE].T.astype(BF16)
    cs = jnp.concatenate(cs, axis=0).astype(BF16)
    for g in range(2):
        cg = cs[:, g * N : (g + 1) * N]
        cc_ref[g] = jnp.concatenate([cg, cg], axis=1)
        lines = []
        for r in range(rows):
            b = bs[r][:, g * N : (g + 1) * N]
            zero = jnp.zeros((2 * STEPS, N), F32)
            mine = jnp.concatenate([b, b], axis=0)
            lines.append(
                jnp.concatenate([mine if q == r else zero for q in range(rows)], axis=1)
            )
        bb_ref[g] = jnp.concatenate(lines, axis=0).astype(BF16)


def core_kernel(
    sizes,
    x_hbm,
    b_hbm,
    c_hbm,
    d_hbm,
    sx_hbm,
    sb_hbm,
    sc_hbm,
    sd_hbm,
    out_hbm,
    g_hbm,
    pre_hbm,
    reach_hbm,
    push_hbm,
    last_hbm,
    cc_hbm,
    bb_hbm,
    xv,
    bv,
    cv,
    dv,
    sx_ref,
    sb_ref,
    sc_ref,
    sd_ref,
    out_ref,
    g_ref,
    pre_ref,
    reach_ref,
    push_ref,
    last_ref,
    cc_ref,
    bb_ref,
    spread_ref,
    bt,
    part,
    state,
    cum,
    cum_t,
    grown,
    remain,
    s_ref,
    e_ref,
    first,
    joined,
    ranks,
    starts,
    tops,
    down,
    onward,
    turned,
    x_sem,
    in_sem,
    out_sem,
    g_sem,
    table_sem,
    up_send,
    up_recv,
    join_send,
    join_recv,
    y_send,
    y_recv,
    down_send,
    down_recv,
    fz_send,
    fz_recv,
    fy_send,
    fy_recv,
    fc_send,
    fc_recv,
):
    nz, ny = sizes
    length, wide = xv.shape
    heads = dv.shape[0]
    groups = bv.shape[1] // N
    per = heads // groups
    blocks = length // B
    s, t, d = lax.axis_index("seq"), lax.axis_index("tp"), lax.axis_index("dp")
    y, z = s // nz, s % nz
    zl, core = d // 2, d % 2
    away = t != d

    def x_load(n):
        at = pl.ds(pl.multiple_of(n * 4 * P_SIZE, 4 * P_SIZE), 4 * P_SIZE)
        return pltpu.make_async_copy(x_hbm.at[:, at], xv.at[:, at], x_sem.at[n])

    loads = [
        pltpu.make_async_copy(src, dst, in_sem.at[n])
        for n, (src, dst) in enumerate(
            (
                (d_hbm, dv), (b_hbm, bv), (c_hbm, cv), (sx_hbm, sx_ref), (sb_hbm, sb_ref),
                (sc_hbm, sc_ref), (sd_hbm, sd_ref),
            )
        )
    ]
    tables = [
        pltpu.make_async_copy(src, dst, table_sem.at[n])
        for n, (src, dst) in enumerate(
            (
                (pre_ref, pre_hbm), (reach_ref, reach_hbm), (push_ref, push_hbm),
                (last_ref, last_hbm), (cc_ref, cc_hbm), (bb_ref, bb_hbm),
            )
        )
    ]

    def y_store(pair):
        at = pair_lanes(pair)
        return pltpu.make_async_copy(out_ref.at[:, at], out_hbm.at[:, at], out_sem.at[pair])

    def g_store(c):
        return pltpu.make_async_copy(g_ref.at[c], g_hbm.at[c], g_sem.at[c])

    loads[0].start()
    loads[1].start()
    for half in range(2):
        for q in range(nz):
            x_load(2 * q + half).start()
    for load in loads[2:]:
        load.start()
    spread_ref[...] = spread_matrix(spread_ref.shape)

    def z_dev(i):
        return (y * nz + (z + i) % nz, t, d)

    def y_dev(i):
        return (((y + i) % ny) * nz + z, t, d)

    def cross_dev(i, l):
        return (y * nz + (z + i) % nz, d, (zl + l) % 2 * 2 + t % 2)

    core_dev = (s, t, zl * 2 + 1 - core)

    def own_source(i, p):
        return jnp.logical_and(d == t, p == t // 2) if i == 0 else False

    barrier = pltpu.get_barrier_semaphore()
    others = [z_dev(1), z_dev(nz - 1)] + [y_dev(i) for i in range(1, ny)] + [core_dev]
    for dev in others:
        pl.semaphore_signal(barrier, inc=1, device_id=dev, device_id_type=MESH)
    for i in range(nz):
        for p in range(2):
            prompt = 2 * p + core

            @pl.when(jnp.logical_not(own_source(i, p)))
            def _():
                pl.semaphore_signal(
                    barrier, inc=1, device_id=(y * nz + (z + i) % nz, prompt, t),
                    device_id_type=MESH,
                )

    count = len(others) + 2 * nz
    pl.semaphore_wait(barrier, jnp.where(away, count, count - 1))

    def copy(src, dst, send, recv, dev):
        return pltpu.make_async_remote_copy(
            src_ref=src, dst_ref=dst, send_sem=send, recv_sem=recv, device_id=dev,
            device_id_type=MESH,
        )

    def turn(q, c):
        return (0, 1, 1 - c % 2, 0)[q]

    def place(q, c):
        j = (z + nz - q) % nz
        return j + turn(q, c) * (3 - 2 * j)

    def near(q, c, step):
        return z_dev(nz + step * (1 - 2 * turn(q, c)))

    def order(q, c):
        f = turn(q, c)
        return ((1, 0, 2), (2, 0, 1), (2 - 2 * f, 1, 2 * f), (0, 2, 1))[q]

    def end_copy(q, c):
        return copy(
            s_ref.at[CH * q + c], ranks.at[q, c, order(q, c)[1]], up_send.at[q, c],
            up_recv.at[q, c], near(q, c, 1),
        )

    def far_copy(q, c):
        return copy(
            s_ref.at[CH * q + c], first.at[q, c], up_send.at[q, c], up_recv.at[q, c],
            near(q, c, -1),
        )

    def join_copy(q, c):
        return copy(
            joined.at[q, c], ranks.at[q, c, order(q, c)[2]], join_send.at[q, c],
            join_recv.at[q, c], near(q, c, -1),
        )

    def y_copy(q, c, i):
        return copy(
            tops.at[q, c, y], tops.at[q, c, y], y_send.at[q, c, i - 1], y_recv.at[q, c, i - 1],
            y_dev(i),
        )

    def down_copy(q, c, n):
        return copy(
            starts.at[q, c, order(q, c)[1 + n]], down.at[q, c], down_send.at[q, c, n],
            down_recv.at[q, c], near(q, c, 2 * n - 1),
        )

    def onward_copy(q, c):
        return copy(
            onward.at[q, c], down.at[q, c], down_send.at[q, c, 0], down_recv.at[q, c],
            near(q, c, 1),
        )

    def fz_copy(q, c, i, l):
        return copy(
            turned.at[q, c, pl.ds(32 * y, 32)], g_ref.at[c, y, t % 2, t // 2, q],
            fz_send.at[q, c, i + nz * l], fz_recv.at[q, c, t // 2], cross_dev(i, l),
        )

    def fz_wait(q, c, p):
        ref = g_ref.at[c, y, core, p, q]
        copy(ref, ref, fz_send.at[q, c, 0], fz_recv.at[q, c, p], core_dev).wait_recv()

    def fy_copy(c, i):
        ref = g_ref.at[c, y, core]
        return copy(ref, ref, fy_send.at[c, i - 1], fy_recv.at[c, i - 1], y_dev(i))

    def fc_copy(c, i):
        ref = g_ref.at[c, (y + ny - i) % ny, core]
        return copy(ref, ref, fc_send.at[c, i], fc_recv.at[c, i], core_dev)

    loads[0].wait()
    row = lax.broadcasted_iota(jnp.int32, (B, B), 0)
    col = lax.broadcasted_iota(jnp.int32, (B, B), 1)
    upper = (row <= col).astype(F32).astype(BF16)
    lead = jnp.zeros((1, 2 * heads), F32)
    leads = []
    rows_of = []
    for k in range(blocks):
        dec = dv[:, k * B : (k + 1) * B] * LOG2E
        hi = dec.astype(BF16)
        mid = (dec - hi.astype(F32)).astype(BF16)
        low = (dec - hi.astype(F32) - mid.astype(F32)).astype(BF16)
        three = jnp.concatenate([hi, mid, low], axis=1)
        rows_of += [three, three]
    sums = dot(jnp.concatenate(rows_of, axis=0), jnp.concatenate([upper] * 3, axis=0))
    for k in range(blocks):
        at = pl.ds(k * B, B)
        mine = sums[k * 2 * heads : (k + 1) * 2 * heads]
        cum[:, at] = mine
        cum_t[at, :] = mine.T
        leads.append(lead)
        lead = lead + cum_t[k * B + B - 1 : k * B + B, :]
    for k in range(blocks):
        at = pl.ds(k * B, B)
        whole = cum_t[at, :] + leads[k]
        remain[at, :] = hi_low(jnp.exp2(jnp.minimum(lead - whole, 0.0)))
    keep = hi_low(jnp.broadcast_to(jnp.exp2(lead), (16, 2 * heads)))

    loads[1].wait()
    for k in range(blocks):
        for g in range(groups):
            at = pl.ds(k * B, B)
            bt[g, :, at] = bv[at, g * N : (g + 1) * N].T

    def at_place(q, c, where, act):
        @pl.when(place(q, c) == where)
        def _():
            act()

    def own_state(half, carry):
        left = remain[...]
        for q in range(nz):
            g = q * CH * 2 // per
            x_load(2 * q + half).wait()
            at = pl.ds(pl.multiple_of((2 * q + half) * 4 * P_SIZE, 4 * P_SIZE), 4 * P_SIZE)
            sp = spread_ref[:, at]
            scaled = (xv[:, at].astype(F32) * dot(left, sp)).astype(BF16)
            both = dot(bt[g], scaled)
            fades = dot(keep, sp)
            for n in range(2):
                c = 2 * half + n
                pair = CH * q + c
                here = slice(n * 2 * P_SIZE, (n + 1) * 2 * P_SIZE)
                s_ref[pair, 0:N] = both[:, here]
                s_ref[pair, N : N + 8] = fades[0:8, here]
                at_place(q, c, 0, lambda: end_copy(q, c).start())
                at_place(q, c, 3, lambda: far_copy(q, c).start())

                @pl.when(place(q, c) == 1)
                def _():
                    ranks[q, c, order(q, c)[0]] = s_ref[pair]

        return carry

    lax.fori_loop(0, 2, own_state, 0)
    for load in loads[2:]:
        load.wait()
    for k in range(blocks):
        at = pl.ds(k * B, B)
        grown[at, :] = hi_low(jnp.exp2(cum_t[at, :] + leads[k]))
    state[...] = jnp.zeros((N, wide), F32)
    lane = lax.broadcasted_iota(jnp.int32, (B, 2 * P_SIZE), 1)

    def block(k):
        rows = pl.ds(pl.multiple_of(k * B, B), B)
        sums, sums_t = cum[:, rows], cum_t[rows, :]
        last = sums_t[B - 1 : B, :]
        grow = hi_low(jnp.exp2(sums_t))
        left = hi_low(jnp.exp2(last - sums_t))
        fade = hi_low(jnp.broadcast_to(jnp.exp2(last), (16, 2 * heads)))
        for g in range(groups):
            lanes = pl.ds(g * per * P_SIZE, per * P_SIZE)
            sp = spread_ref[:, lanes]
            c = cv[rows, g * N : (g + 1) * N]
            x = xv[rows, lanes]
            before = state[:, lanes]
            carried = dot(c, before.astype(BF16)) * dot(grow, sp)
            scaled = (x.astype(F32) * dot(left, sp)).astype(BF16)
            term = dot(bt[g, :, rows], scaled)
            state[:, lanes] = before * dot(fade, sp)[0:1, :] + term
            scores = jnp.where(row >= col, dot(c, bt[g, :, rows]), 0.0)
            for n in range(per // 2):
                weights = []
                for h in (g * per + 2 * n, g * per + 2 * n + 1):
                    gap = jnp.minimum(sums_t[:, h : h + 1] - sums[h : h + 1, :], 0.0)
                    weights.append((scores * jnp.exp2(gap)).astype(BF16))
                here = slice(n * 2 * P_SIZE, (n + 1) * 2 * P_SIZE)
                zero = jnp.zeros((B, 2 * P_SIZE), BF16)
                both = jnp.concatenate(
                    [
                        jnp.where(lane < P_SIZE, x[:, here], zero),
                        jnp.where(lane < P_SIZE, zero, x[:, here]),
                    ],
                    axis=0,
                )
                inner = dot(jnp.concatenate(weights, axis=1), both)
                part[rows, pl.ds((g * per + 2 * n) * P_SIZE, 2 * P_SIZE)] = inner + carried[:, here]

    def join(q, c):
        far_copy(q, c).wait_recv()
        pair = CH * q + c
        f = turn(q, c) == 1
        own, other = s_ref[pair, 0:N], first[q, c, 0:N]
        keep, fade = s_ref[pair, N : N + 8], first[q, c, N : N + 8]
        joined[q, c, 0:N] = jnp.where(f, other, own) * jnp.where(f, keep[0:1], fade[0:1]) + (
            jnp.where(f, own, other)
        )
        joined[q, c, N : N + 8] = keep * fade
        join_copy(q, c).start()

    def gather(q, c):
        end_copy(q, c).wait_recv()
        join_copy(q, c).wait_recv()
        top = ranks[q, c, 0, 0:N]
        kept = ranks[q, c, 0, N : N + 8]
        for k in range(1, 3):
            a = ranks[q, c, k, N : N + 8]
            top = top * a[0:1] + ranks[q, c, k, 0:N]
            kept = kept * a
        tops[q, c, y, 0:N] = top
        tops[q, c, y, N : N + 8] = kept
        for i in range(1, ny):
            y_copy(q, c, i).start()

    def spread_out(q, c):
        for i in range(1, ny):
            y_copy(q, c, i).wait_recv()
        enter = jnp.zeros((N, 2 * P_SIZE), F32)
        last = enter
        for k in range(ny):
            a = tops[q, c, k, N : N + 1]
            top = tops[q, c, k, 0:N]
            enter = jnp.where(k < y, enter * a + top, enter)
            last = last * a + top
        turned[q, c] = last.T
        for k in range(3):
            starts[q, c, k] = enter
            if k < 2:
                enter = enter * ranks[q, c, k, N : N + 1] + ranks[q, c, k, 0:N]
        for l in range(2):
            for i in range(nz):
                if i or l:
                    fz_copy(q, c, i, l).start()

        @pl.when(away)
        def _():
            fz_copy(q, c, 0, 0).start()

        @pl.when(jnp.logical_not(away))
        def _():
            g_ref[c, y, core, zl, q] = turned[q, c, pl.ds(32 * y, 32)]

        for n in (1, 0):
            down_copy(q, c, n).start()
        e_ref[CH * q + c] = starts[q, c, order(q, c)[0]]

    def pass_on(q, c):
        down_copy(q, c, 1).wait_recv()
        pair = CH * q + c
        f = turn(q, c) == 1
        came = down[q, c]
        own, other = s_ref[pair, 0:N], first[q, c, 0:N]
        a = jnp.where(f, first[q, c, N : N + 1], s_ref[pair, N : N + 1])
        after = came * a + jnp.where(f, other, own)
        onward[q, c] = jnp.where(f, came, after)
        onward_copy(q, c).start()
        e_ref[pair] = jnp.where(f, after, came)

    def arrive(q, c):
        @pl.when(place(q, c) % 3 == 0)
        def _():
            onward_copy(q, c).wait_recv()
            e_ref[CH * q + c] = down[q, c]

    def each(act, where):
        def stage(c):
            for q in range(nz):
                at_place(q, c, where, functools.partial(act, q, c))

        return stage

    def stage_e(c):
        for q in range(nz):
            for p in range(2):
                mine = jnp.logical_and(place(q, c) == 1, jnp.logical_and(d == t, p == t // 2))

                @pl.when(jnp.logical_not(mine))
                def _():
                    fz_wait(q, c, p)

        for i in range(1, ny):
            fy_copy(c, i).start()
        fc_copy(c, 0).start()

    def stage_d(c):
        for i in range(1, ny):
            fy_copy(c, i).wait_recv()
            fc_copy(c, i).start()

    def stage_f(c):
        for i in range(ny):
            fc_copy(c, i).wait_recv()
        g_store(c).start()

    def close(c):
        for q in range(nz):
            arrive(q, c)
        for q in range(nz):
            pair = CH * q + c
            g = q * CH * 2 // per
            at = pair_lanes(pair)
            carried = dot(cv[:, g * N : (g + 1) * N], e_ref[pair].astype(BF16))
            carried = carried * dot(grown[...], spread_ref[:, at])
            out_ref[:, at] = (part[:, at] + carried).astype(BF16)
            y_store(pair).start()

    stages = (
        (each(join, 2), 0), (each(gather, 1), 1), (each(spread_out, 1), 2), (stage_e, 4),
        (each(pass_on, 2), 4), (stage_d, 6), (stage_f, 7),
    )
    def step(n, carry):
        for stage, after in stages:

            @pl.when(jnp.logical_and(n >= after, n < after + CH))
            def _():
                stage(n - after)

        @pl.when(n < blocks)
        def _():
            block(n)

        @pl.when(n == TABLES)
        def _():
            decode_tables(
                sx_ref, sb_ref, sc_ref, sd_ref, spread_ref, pre_ref, reach_ref, push_ref,
                last_ref, cc_ref, bb_ref,
            )
            for table in tables:
                table.start()

        @pl.when(n >= CLOSE)
        def _():
            close(n - CLOSE)

        return carry

    lax.fori_loop(0, CLOSE + CH, step, 0)

    def drain(c, carry):
        for q in range(nz):
            at_place(q, c, 0, lambda: end_copy(q, c).wait_send())
            at_place(q, c, 3, lambda: far_copy(q, c).wait_send())

            @pl.when(place(q, c) == 1)
            def _():
                for n in range(2):
                    down_copy(q, c, n).wait_send()
                for i in range(1, ny):
                    y_copy(q, c, i).wait_send()
                for l in range(2):
                    for i in range(nz):
                        if i or l:
                            fz_copy(q, c, i, l).wait_send()

                @pl.when(away)
                def _():
                    fz_copy(q, c, 0, 0).wait_send()

            @pl.when(place(q, c) == 2)
            def _():
                join_copy(q, c).wait_send()
                onward_copy(q, c).wait_send()

            y_store(CH * q + c).wait()
        for i in range(1, ny):
            fy_copy(c, i).wait_send()
        for i in range(ny):
            fc_copy(c, i).wait_send()
        g_store(c).wait()
        return carry

    lax.fori_loop(0, CH, drain, 0)
    for table in tables:
        table.wait()


CLOSE = 7
TABLES = 8


def core(x, b, c, decay, sx, sb, sc, sd, nz, ny):
    length, wide = x.shape
    heads = decay.shape[0]
    pairs = heads // 2
    rows = sx.shape[1]
    dma = pltpu.SemaphoreType.DMA
    hbm = pl.BlockSpec(memory_space=pl.ANY)
    pair_shape = (N, 2 * P_SIZE)
    outs = (
        jax.ShapeDtypeStruct(x.shape, BF16),
        jax.ShapeDtypeStruct((CH, ny, 2, 2, nz, 32, N), F32),
        jax.ShapeDtypeStruct((rows, STEPS, wide), F32),
        jax.ShapeDtypeStruct((rows, STEPS, wide), F32),
        jax.ShapeDtypeStruct((wide, 2 * STEPS * rows), BF16),
        jax.ShapeDtypeStruct((rows, heads, N), F32),
        jax.ShapeDtypeStruct((2, rows * STEPS, 2 * N), BF16),
        jax.ShapeDtypeStruct((2, 2 * STEPS * rows, rows * N), BF16),
    )
    return pl.pallas_call(
        functools.partial(core_kernel, (nz, ny)),
        out_shape=outs,
        in_specs=[hbm] * 8,
        out_specs=(hbm,) * len(outs),
        scratch_shapes=[
            pltpu.VMEM(x.shape, BF16),
            pltpu.VMEM(b.shape, BF16),
            pltpu.VMEM(c.shape, BF16),
            pltpu.VMEM(decay.shape, F32),
            pltpu.VMEM(sx.shape, BF16),
            pltpu.VMEM(sb.shape, BF16),
            pltpu.VMEM(sc.shape, BF16),
            pltpu.VMEM(sd.shape, F32),
        ]
        + [pltpu.VMEM(out.shape, out.dtype) for out in outs]
        + [
            pltpu.VMEM((2 * heads, wide), BF16),
            pltpu.VMEM((2, N, length), BF16),
            pltpu.VMEM(x.shape, F32),
            pltpu.VMEM((N, wide), F32),
            pltpu.VMEM((2 * heads, length), F32),
            pltpu.VMEM((length, 2 * heads), F32),
            pltpu.VMEM((length, 2 * heads), BF16),
            pltpu.VMEM((length, 2 * heads), BF16),
            pltpu.VMEM((pairs, N + 8, 2 * P_SIZE), F32),
            pltpu.VMEM((pairs,) + pair_shape, F32),
            pltpu.VMEM((nz, CH, N + 8, 2 * P_SIZE), F32),
            pltpu.VMEM((nz, CH, N + 8, 2 * P_SIZE), F32),
            pltpu.VMEM((nz, CH, 3, N + 8, 2 * P_SIZE), F32),
            pltpu.VMEM((nz, CH, 3) + pair_shape, F32),
            pltpu.VMEM((nz, CH, ny, N + 8, 2 * P_SIZE), F32),
            pltpu.VMEM((nz, CH) + pair_shape, F32),
            pltpu.VMEM((nz, CH) + pair_shape, F32),
            pltpu.VMEM((nz, CH, 2 * P_SIZE, N), F32),
            dma((2 * nz,)),
            dma((7,)),
            dma((pairs,)),
            dma((CH,)),
            dma((6,)),
            dma((nz, CH)), dma((nz, CH)),
            dma((nz, CH)), dma((nz, CH)),
            dma((nz, CH, 3)), dma((nz, CH, 3)),
            dma((nz, CH, 2)), dma((nz, CH)),
            dma((nz, CH, 8)), dma((nz, CH, 2)),
            dma((CH, 3)), dma((CH, 3)),
            dma((CH, 4)), dma((CH, 4)),
        ],
        compiler_params=pltpu.CompilerParams(
            collective_id=0, has_side_effects=True, vmem_limit_bytes=60 * MIB
        ),
        name="core",
    )(x, b, c, decay, sx, sb, sc, sd)


def decode_kernel(
    row_ref, slot_ref, y_hbm, g_hbm, *rest
):
    tables_hbm, rest = rest[:6], rest[6:]
    y_out, out_hbm, cache_hbm, y_ref, g_ref = rest[:5]
    tables, rest = rest[5:11], rest[11:]
    pre_ref, reach_ref, push_ref, last_ref, cc_ref, bb_ref = tables
    out_ref, cache_ref, load_sem, y_load_sem, y_sem, g_sem, out_sem, cache_sem = rest
    rows = pre_ref.shape[0]
    loads = [
        pltpu.make_async_copy(src, dst, load_sem.at[n])
        for n, (src, dst) in enumerate(zip(tables_hbm, tables))
    ]

    def g_load(chunk):
        return pltpu.make_async_copy(g_hbm.at[chunk], g_ref.at[chunk], g_sem.at[chunk])

    height = y_ref.shape[0] // CH

    def y_load(n):
        at = pl.ds(pl.multiple_of(n * height, height), height)
        return pltpu.make_async_copy(y_hbm.at[at], y_ref.at[at], y_load_sem.at[n])

    def y_store(n):
        at = pl.ds(pl.multiple_of(n * height, height), height)
        return pltpu.make_async_copy(y_ref.at[at], y_out.at[at], y_sem.at[n])

    for load in loads:
        load.start()
    g_load(0).start()
    g_load(1).start()
    for n in range(CH):
        y_load(n).start()
    for n in range(2, CH):
        g_load(n).start()
    for load in loads:
        load.wait()

    def cache_store(chunk):
        return pltpu.make_async_copy(
            cache_ref.at[chunk], cache_hbm.at[:, :, chunk], cache_sem.at[chunk]
        )

    def work(chunk, carry):
        g_load(chunk).wait()
        for zi in range(4):
            g = zi // 2
            pair = CH * zi + chunk
            at = pair_lanes(pair)
            seen = []
            for prompt in range(4):
                f = g_ref[chunk, :, prompt % 2, prompt // 2, zi].reshape(2 * P_SIZE, N)
                hi = f.astype(BF16)
                low = (f - hi.astype(F32)).astype(BF16)
                seen.append(dot(cc_ref[g], jnp.concatenate([hi, low], axis=1), ((1,), (1,))))
            gain = dot(push_ref[at, :], bb_ref[g])
            for r in range(rows):
                mine = row_ref[r]
                part = slice(r * STEPS, (r + 1) * STEPS)
                pick = seen[0][part]
                for prompt in range(1, 4):
                    pick = jnp.where(mine == prompt, seen[prompt][part], pick)
                out_ref[:, r, at] = (pick * reach_ref[r, :, at] + pre_ref[r, :, at]).astype(BF16)
                f = g_ref[chunk, :, mine % 2, mine // 2, zi].reshape(2 * P_SIZE, N)
                kept = jnp.concatenate(
                    [
                        jnp.broadcast_to(last_ref[r, pl.ds(2 * pair + n, 1), :], (P_SIZE, N))
                        for n in range(2)
                    ],
                    axis=0,
                )
                cache_ref[chunk, slot_ref[r], zi] = (
                    f * kept + gain[:, r * N : (r + 1) * N]
                ).astype(BF16)
        cache_store(chunk).start()
        y_load(chunk).wait()
        y_store(chunk).start()
        return carry

    lax.fori_loop(0, CH, work, 0)
    out_store = pltpu.make_async_copy(out_ref, out_hbm, out_sem)
    out_store.start()
    for chunk in range(CH):
        y_store(chunk).wait()
        cache_store(chunk).wait()
    out_store.wait()


def decode(row_prompt, cache_slot, y, g, tables, shape):
    rows = shape[1]
    nz = g.shape[4]
    heads = shape[2] // P_SIZE
    smem = pl.BlockSpec(memory_space=pltpu.SMEM)
    hbm = pl.BlockSpec(memory_space=pl.ANY)
    dma = pltpu.SemaphoreType.DMA
    seq, out, cache = pl.pallas_call(
        decode_kernel,
        out_shape=(
            jax.ShapeDtypeStruct(y.shape, BF16),
            jax.ShapeDtypeStruct(shape, BF16),
            jax.ShapeDtypeStruct((rows, nz, CH, 2 * P_SIZE, N), BF16),
        ),
        in_specs=[smem, smem] + [hbm] * (2 + len(tables)),
        out_specs=(hbm, hbm, hbm),
        scratch_shapes=[pltpu.VMEM(a.shape, a.dtype) for a in (y, g, *tables)]
        + [
            pltpu.VMEM(shape, BF16),
            pltpu.VMEM((CH, rows, nz, 2 * P_SIZE, N), BF16),
            dma((len(tables),)),
            dma((CH,)),
            dma((CH,)),
            dma((CH,)),
            dma(()),
            dma((CH,)),
        ],
        compiler_params=pltpu.CompilerParams(vmem_limit_bytes=60 * MIB),
        name="decode",
    )(row_prompt, cache_slot, y, g, *tables)
    return seq, out, cache.reshape(rows, heads, P_SIZE, N)


def per_device(x, b, c, decay, row_prompt, cache_slot, step_x, step_b, step_c, step_decay):
    nz, ny = 4, lax.axis_size("seq") // 4
    y, g, *tables = core(
        x[0], b[0], c[0], decay[0], step_x, step_b, step_c, step_decay, nz, ny
    )
    seq, out, cache = decode(row_prompt, cache_slot, y, g, tables, step_x.shape)
    return seq[None], out, cache


def solution(mesh):
    return jax.shard_map(
        per_device,
        mesh=mesh,
        in_specs=(
            P("tp", "seq", "dp"),
            P("tp", "seq", "dp"),
            P("tp", "seq", "dp"),
            P("tp", "dp", "seq"),
            P(("seq", "dp")),
            P(("seq", "dp")),
            P(None, ("seq", "dp"), "tp"),
            P(None, ("seq", "dp"), "tp"),
            P(None, ("seq", "dp"), "tp"),
            P(None, ("seq", "dp"), "tp"),
        ),
        out_specs=(
            P("tp", "seq", "dp"),
            P(None, ("seq", "dp"), "tp"),
            P(("seq", "dp"), "tp", None, None),
        ),
        check_vma=False,
    )
```

```python
import functools
import math

import jax
import jax.numpy as jnp
from jax import lax
from jax.experimental import pallas as pl
from jax.experimental.pallas import tpu as pltpu
from jax.sharding import PartitionSpec as P

MESH = pl.DeviceIdType.MESH
P_SIZE = 64
N = 128
B = 128
STEPS = 8
LOG2E = math.log2(math.e)
F32 = jnp.float32
BF16 = jnp.bfloat16
CH = 4
MIB = 2**20


def dot(a, b, dims=((1,), (0,)), precision=None):
    return lax.dot_general(
        a, b, (dims, ((), ())), preferred_element_type=F32, precision=precision
    )


def spread_matrix(shape):
    heads = shape[0] // 2
    row = lax.broadcasted_iota(jnp.int32, shape, 0)
    lane = lax.broadcasted_iota(jnp.int32, shape, 1)
    return (row % heads == lane // P_SIZE).astype(F32).astype(BF16)


def pair_lanes(pair):
    return pl.ds(pl.multiple_of(pair * 2 * P_SIZE, 2 * P_SIZE), 2 * P_SIZE)


def hi_low(v):
    hi = v.astype(BF16)
    lane = lax.broadcasted_iota(jnp.int32, v.shape, 1)
    return jnp.where(lane < v.shape[1] // 2, hi, (v - hi.astype(F32)).astype(BF16))


def decode_tables(x_ref, b_ref, c_ref, d_ref, spread_ref, pre_ref, reach_ref, push_ref, last_ref, cc_ref, bb_ref):
    rows, heads = d_ref.shape[1], d_ref.shape[2]
    lane = lax.broadcasted_iota(jnp.int32, (STEPS * STEPS, heads), 1)
    x_all = x_ref[...].astype(F32)
    b_all = b_ref[...].astype(F32)
    c_all = c_ref[...].astype(F32)
    pushes, cs, bs = [], [], []
    for r in range(rows):
        keep = d_ref[:, r, :]
        x, b, c = x_all[:, r, :], b_all[:, r, :], c_all[:, r, :]
        grid = []
        for k in range(STEPS):
            line = [jnp.zeros((1, heads), F32)] * k + [jnp.ones((1, heads), F32)]
            for s in range(k + 1, STEPS):
                line.append(line[-1] * keep[s : s + 1])
            grid.append(jnp.concatenate(line, axis=0))
        line = [keep[0:1]]
        for s in range(1, STEPS):
            line.append(line[-1] * keep[s : s + 1])
        meet = []
        for g in range(2):
            bg, cg = b[:, g * N : (g + 1) * N], c[:, g * N : (g + 1) * N]
            meet.append(
                jnp.concatenate(
                    [jnp.sum(cg * bg[k : k + 1], axis=1, keepdims=True) for k in range(STEPS)],
                    axis=0,
                )
            )
        met = jnp.concatenate(grid, axis=0) * jnp.where(lane < heads // 2, meet[0], meet[1])
        left = [grid[k][STEPS - 1 : STEPS] for k in range(STEPS)]
        table = jnp.concatenate([met] + line + left, axis=0)
        co = dot(hi_low(jnp.concatenate([table, table], axis=1)), spread_ref[...])
        base = STEPS * STEPS
        local = co[0:STEPS] * x[0:1]
        for k in range(1, STEPS):
            local += co[k * STEPS : (k + 1) * STEPS] * x[k : k + 1]
        pre_ref[r] = local
        reach_ref[r] = co[base : base + STEPS]
        push = x * co[base + STEPS : base + 2 * STEPS]
        hi = push.astype(BF16).astype(F32)
        pushes += [hi, push - hi]
        last_ref[r] = jnp.broadcast_to(line[-1], (N, heads)).T
        cs.append(c)
        bs.append(b)
    pushes = jnp.concatenate(pushes, axis=0)
    for pair in range(heads // 2):
        at = pl.ds(pair * 2 * P_SIZE, 2 * P_SIZE)
        push_ref[at, :] = pushes[:, pair * 2 * P_SIZE : (pair + 1) * 2 * P_SIZE].T.astype(BF16)
    cs = jnp.concatenate(cs, axis=0).astype(BF16)
    for g in range(2):
        cg = cs[:, g * N : (g + 1) * N]
        cc_ref[g] = jnp.concatenate([cg, cg], axis=1)
        lines = []
        for r in range(rows):
            b = bs[r][:, g * N : (g + 1) * N]
            zero = jnp.zeros((2 * STEPS, N), F32)
            mine = jnp.concatenate([b, b], axis=0)
            lines.append(
                jnp.concatenate([mine if q == r else zero for q in range(rows)], axis=1)
            )
        bb_ref[g] = jnp.concatenate(lines, axis=0).astype(BF16)


def core_kernel(
    sizes,
    x_hbm,
    b_hbm,
    c_hbm,
    d_hbm,
    sx_hbm,
    sb_hbm,
    sc_hbm,
    sd_hbm,
    out_hbm,
    g_hbm,
    pre_hbm,
    reach_hbm,
    push_hbm,
    last_hbm,
    cc_hbm,
    bb_hbm,
    xv,
    bv,
    cv,
    dv,
    sx_ref,
    sb_ref,
    sc_ref,
    sd_ref,
    out_ref,
    g_ref,
    pre_ref,
    reach_ref,
    push_ref,
    last_ref,
    cc_ref,
    bb_ref,
    spread_ref,
    bt,
    part,
    state,
    cum,
    cum_t,
    grown,
    remain,
    s_ref,
    e_ref,
    first,
    joined,
    ranks,
    starts,
    tops,
    down,
    onward,
    turned,
    x_sem,
    in_sem,
    out_sem,
    g_sem,
    table_sem,
    up_send,
    up_recv,
    join_send,
    join_recv,
    y_send,
    y_recv,
    down_send,
    down_recv,
    fz_send,
    fz_recv,
    fy_send,
    fy_recv,
    fc_send,
    fc_recv,
):
    nz, ny = sizes
    length, wide = xv.shape
    heads = dv.shape[0]
    groups = bv.shape[1] // N
    per = heads // groups
    blocks = length // B
    s, t, d = lax.axis_index("seq"), lax.axis_index("tp"), lax.axis_index("dp")
    y, z = s // nz, s % nz
    zl, core = d // 2, d % 2
    away = t != d

    def x_load(n):
        at = pl.ds(pl.multiple_of(n * 4 * P_SIZE, 4 * P_SIZE), 4 * P_SIZE)
        return pltpu.make_async_copy(x_hbm.at[:, at], xv.at[:, at], x_sem.at[n])

    loads = [
        pltpu.make_async_copy(src, dst, in_sem.at[n])
        for n, (src, dst) in enumerate(
            (
                (d_hbm, dv), (b_hbm, bv), (c_hbm, cv), (sx_hbm, sx_ref), (sb_hbm, sb_ref),
                (sc_hbm, sc_ref), (sd_hbm, sd_ref),
            )
        )
    ]
    tables = [
        pltpu.make_async_copy(src, dst, table_sem.at[n])
        for n, (src, dst) in enumerate(
            (
                (pre_ref, pre_hbm), (reach_ref, reach_hbm), (push_ref, push_hbm),
                (last_ref, last_hbm), (cc_ref, cc_hbm), (bb_ref, bb_hbm),
            )
        )
    ]

    def y_store(pair):
        at = pair_lanes(pair)
        return pltpu.make_async_copy(out_ref.at[:, at], out_hbm.at[:, at], out_sem.at[pair])

    def g_store(c):
        return pltpu.make_async_copy(g_ref.at[c], g_hbm.at[c], g_sem.at[c])

    loads[0].start()
    loads[1].start()
    for half in range(2):
        for q in range(nz):
            x_load(2 * q + half).start()
    for load in loads[2:]:
        load.start()
    spread_ref[...] = spread_matrix(spread_ref.shape)

    def z_dev(i):
        return (y * nz + (z + i) % nz, t, d)

    def y_dev(i):
        return (((y + i) % ny) * nz + z, t, d)

    def cross_dev(i, l):
        return (y * nz + (z + i) % nz, d, (zl + l) % 2 * 2 + t % 2)

    core_dev = (s, t, zl * 2 + 1 - core)

    def own_source(i, p):
        return jnp.logical_and(d == t, p == t // 2) if i == 0 else False

    barrier = pltpu.get_barrier_semaphore()
    others = [z_dev(1), z_dev(nz - 1)] + [y_dev(i) for i in range(1, ny)] + [core_dev]
    for dev in others:
        pl.semaphore_signal(barrier, inc=1, device_id=dev, device_id_type=MESH)
    for i in range(nz):
        for p in range(2):
            prompt = 2 * p + core

            @pl.when(jnp.logical_not(own_source(i, p)))
            def _():
                pl.semaphore_signal(
                    barrier, inc=1, device_id=(y * nz + (z + i) % nz, prompt, t),
                    device_id_type=MESH,
                )


    def copy(src, dst, send, recv, dev):
        return pltpu.make_async_remote_copy(
            src_ref=src, dst_ref=dst, send_sem=send, recv_sem=recv, device_id=dev,
            device_id_type=MESH,
        )

    def turn(q, c):
        return (0, 1, 1 - c % 2, 0)[q]

    def place(q, c):
        j = (z + nz - q) % nz
        return j + turn(q, c) * (3 - 2 * j)

    def near(q, c, step):
        return z_dev(nz + step * (1 - 2 * turn(q, c)))

    def order(q, c):
        f = turn(q, c)
        return ((1, 0, 2), (2, 0, 1), (2 - 2 * f, 1, 2 * f), (0, 2, 1))[q]

    def end_copy(q, c):
        return copy(
            s_ref.at[CH * q + c], ranks.at[q, c, order(q, c)[1]], up_send.at[q, c],
            up_recv.at[q, c], near(q, c, 1),
        )

    def far_copy(q, c):
        return copy(
            s_ref.at[CH * q + c], first.at[q, c], up_send.at[q, c], up_recv.at[q, c],
            near(q, c, -1),
        )

    def join_copy(q, c):
        return copy(
            joined.at[q, c], ranks.at[q, c, order(q, c)[2]], join_send.at[q, c],
            join_recv.at[q, c], near(q, c, -1),
        )

    def y_copy(q, c, i):
        return copy(
            tops.at[q, c, y], tops.at[q, c, y], y_send.at[q, c, i - 1], y_recv.at[q, c, i - 1],
            y_dev(i),
        )

    def down_copy(q, c, n):
        return copy(
            starts.at[q, c, order(q, c)[1 + n]], down.at[q, c], down_send.at[q, c, n],
            down_recv.at[q, c], near(q, c, 2 * n - 1),
        )

    def onward_copy(q, c):
        return copy(
            onward.at[q, c], down.at[q, c], down_send.at[q, c, 0], down_recv.at[q, c],
            near(q, c, 1),
        )

    def fz_copy(q, c, i, l):
        return copy(
            turned.at[q, c, pl.ds(32 * y, 32)], g_ref.at[c, y, t % 2, t // 2, q],
            fz_send.at[q, c, i + nz * l], fz_recv.at[q, c, t // 2], cross_dev(i, l),
        )

    def fz_wait(q, c, p):
        ref = g_ref.at[c, y, core, p, q]
        copy(ref, ref, fz_send.at[q, c, 0], fz_recv.at[q, c, p], core_dev).wait_recv()

    def fy_copy(c, i):
        ref = g_ref.at[c, y, core]
        return copy(ref, ref, fy_send.at[c, i - 1], fy_recv.at[c, i - 1], y_dev(i))

    def fc_copy(c, i):
        ref = g_ref.at[c, (y + ny - i) % ny, core]
        return copy(ref, ref, fc_send.at[c, i], fc_recv.at[c, i], core_dev)

    loads[0].wait()
    row = lax.broadcasted_iota(jnp.int32, (B, B), 0)
    col = lax.broadcasted_iota(jnp.int32, (B, B), 1)
    upper = (row <= col).astype(F32).astype(BF16)
    lead = jnp.zeros((1, 2 * heads), F32)
    leads = []
    rows_of = []
    for k in range(blocks):
        dec = dv[:, k * B : (k + 1) * B] * LOG2E
        hi = dec.astype(BF16)
        mid = (dec - hi.astype(F32)).astype(BF16)
        low = (dec - hi.astype(F32) - mid.astype(F32)).astype(BF16)
        three = jnp.concatenate([hi, mid, low], axis=1)
        rows_of += [three, three]
    sums = dot(jnp.concatenate(rows_of, axis=0), jnp.concatenate([upper] * 3, axis=0))
    for k in range(blocks):
        at = pl.ds(k * B, B)
        mine = sums[k * 2 * heads : (k + 1) * 2 * heads]
        cum[:, at] = mine
        cum_t[at, :] = mine.T
        leads.append(lead)
        lead = lead + cum_t[k * B + B - 1 : k * B + B, :]
    for k in range(blocks):
        at = pl.ds(k * B, B)
        whole = cum_t[at, :] + leads[k]
        remain[at, :] = hi_low(jnp.exp2(jnp.minimum(lead - whole, 0.0)))
    keep = hi_low(jnp.broadcast_to(jnp.exp2(lead), (16, 2 * heads)))

    loads[1].wait()
    for k in range(blocks):
        for g in range(groups):
            at = pl.ds(k * B, B)
            bt[g, :, at] = bv[at, g * N : (g + 1) * N].T

    def at_place(q, c, where, act):
        @pl.when(place(q, c) == where)
        def _():
            act()

    def own_state(half, carry):
        left = remain[...]
        for q in range(nz):
            g = q * CH * 2 // per
            x_load(2 * q + half).wait()
            at = pl.ds(pl.multiple_of((2 * q + half) * 4 * P_SIZE, 4 * P_SIZE), 4 * P_SIZE)
            sp = spread_ref[:, at]
            scaled = (xv[:, at].astype(F32) * dot(left, sp)).astype(BF16)
            both = dot(bt[g], scaled)
            fades = dot(keep, sp)
            for n in range(2):
                c = 2 * half + n
                pair = CH * q + c
                here = slice(n * 2 * P_SIZE, (n + 1) * 2 * P_SIZE)
                s_ref[pair, 0:N] = both[:, here]
                s_ref[pair, N : N + 8] = fades[0:8, here]
                at_place(q, c, 0, lambda: end_copy(q, c).start())
                at_place(q, c, 3, lambda: far_copy(q, c).start())

                @pl.when(place(q, c) == 1)
                def _():
                    ranks[q, c, order(q, c)[0]] = s_ref[pair]

        return carry

    count = len(others) + 2 * nz
    pl.semaphore_wait(barrier, jnp.where(away, count, count - 1))
    lax.fori_loop(0, 2, own_state, 0)
    for load in loads[2:]:
        load.wait()
    for k in range(blocks):
        at = pl.ds(k * B, B)
        grown[at, :] = hi_low(jnp.exp2(cum_t[at, :] + leads[k]))
    state[...] = jnp.zeros((N, wide), F32)
    lane = lax.broadcasted_iota(jnp.int32, (B, 2 * P_SIZE), 1)

    def block(k):
        rows = pl.ds(pl.multiple_of(k * B, B), B)
        sums, sums_t = cum[:, rows], cum_t[rows, :]
        last = sums_t[B - 1 : B, :]
        grow = hi_low(jnp.exp2(sums_t))
        left = hi_low(jnp.exp2(last - sums_t))
        fade = hi_low(jnp.broadcast_to(jnp.exp2(last), (16, 2 * heads)))
        for g in range(groups):
            lanes = pl.ds(g * per * P_SIZE, per * P_SIZE)
            sp = spread_ref[:, lanes]
            c = cv[rows, g * N : (g + 1) * N]
            x = xv[rows, lanes]
            before = state[:, lanes]
            carried = dot(c, before.astype(BF16)) * dot(grow, sp)
            scaled = (x.astype(F32) * dot(left, sp)).astype(BF16)
            term = dot(bt[g, :, rows], scaled)
            state[:, lanes] = before * dot(fade, sp)[0:1, :] + term
            scores = jnp.where(row >= col, dot(c, bt[g, :, rows]), 0.0)
            for n in range(per // 2):
                weights = []
                for h in (g * per + 2 * n, g * per + 2 * n + 1):
                    gap = jnp.minimum(sums_t[:, h : h + 1] - sums[h : h + 1, :], 0.0)
                    weights.append((scores * jnp.exp2(gap)).astype(BF16))
                here = slice(n * 2 * P_SIZE, (n + 1) * 2 * P_SIZE)
                zero = jnp.zeros((B, 2 * P_SIZE), BF16)
                both = jnp.concatenate(
                    [
                        jnp.where(lane < P_SIZE, x[:, here], zero),
                        jnp.where(lane < P_SIZE, zero, x[:, here]),
                    ],
                    axis=0,
                )
                inner = dot(jnp.concatenate(weights, axis=1), both)
                part[rows, pl.ds((g * per + 2 * n) * P_SIZE, 2 * P_SIZE)] = inner + carried[:, here]

    def join(q, c):
        far_copy(q, c).wait_recv()
        pair = CH * q + c
        f = turn(q, c) == 1
        own, other = s_ref[pair, 0:N], first[q, c, 0:N]
        keep, fade = s_ref[pair, N : N + 8], first[q, c, N : N + 8]
        joined[q, c, 0:N] = jnp.where(f, other, own) * jnp.where(f, keep[0:1], fade[0:1]) + (
            jnp.where(f, own, other)
        )
        joined[q, c, N : N + 8] = keep * fade
        join_copy(q, c).start()

    def gather(q, c):
        end_copy(q, c).wait_recv()
        join_copy(q, c).wait_recv()
        top = ranks[q, c, 0, 0:N]
        kept = ranks[q, c, 0, N : N + 8]
        for k in range(1, 3):
            a = ranks[q, c, k, N : N + 8]
            top = top * a[0:1] + ranks[q, c, k, 0:N]
            kept = kept * a
        tops[q, c, y, 0:N] = top
        tops[q, c, y, N : N + 8] = kept
        for i in range(1, ny):
            y_copy(q, c, i).start()

    def spread_out(q, c):
        for i in range(1, ny):
            y_copy(q, c, i).wait_recv()
        enter = jnp.zeros((N, 2 * P_SIZE), F32)
        last = enter
        for k in range(ny):
            a = tops[q, c, k, N : N + 1]
            top = tops[q, c, k, 0:N]
            enter = jnp.where(k < y, enter * a + top, enter)
            last = last * a + top
        turned[q, c] = last.T
        for k in range(3):
            starts[q, c, k] = enter
            if k < 2:
                enter = enter * ranks[q, c, k, N : N + 1] + ranks[q, c, k, 0:N]
        for l in range(2):
            for i in range(nz):
                if i or l:
                    fz_copy(q, c, i, l).start()

        @pl.when(away)
        def _():
            fz_copy(q, c, 0, 0).start()

        @pl.when(jnp.logical_not(away))
        def _():
            g_ref[c, y, core, zl, q] = turned[q, c, pl.ds(32 * y, 32)]

        e_ref[CH * q + c] = starts[q, c, order(q, c)[0]]

    def send_down(q, c):
        for n in (1, 0):
            down_copy(q, c, n).start()

    def pass_on(q, c):
        down_copy(q, c, 1).wait_recv()
        pair = CH * q + c
        f = turn(q, c) == 1
        came = down[q, c]
        own, other = s_ref[pair, 0:N], first[q, c, 0:N]
        a = jnp.where(f, first[q, c, N : N + 1], s_ref[pair, N : N + 1])
        after = came * a + jnp.where(f, other, own)
        onward[q, c] = jnp.where(f, came, after)
        onward_copy(q, c).start()
        e_ref[pair] = jnp.where(f, after, came)

    def arrive(q, c):
        @pl.when(place(q, c) % 3 == 0)
        def _():
            onward_copy(q, c).wait_recv()
            e_ref[CH * q + c] = down[q, c]

    def each(act, where):
        def stage(c):
            for q in range(nz):
                at_place(q, c, where, functools.partial(act, q, c))

        return stage

    def stage_e(c):
        for q in range(nz):
            for p in range(2):
                mine = jnp.logical_and(place(q, c) == 1, jnp.logical_and(d == t, p == t // 2))

                @pl.when(jnp.logical_not(mine))
                def _():
                    fz_wait(q, c, p)

        for i in range(1, ny):
            fy_copy(c, i).start()
        fc_copy(c, 0).start()

    def stage_d(c):
        for i in range(1, ny):
            fy_copy(c, i).wait_recv()
            fc_copy(c, i).start()

    def stage_f(c):
        for i in range(ny):
            fc_copy(c, i).wait_recv()
        g_store(c).start()

    def close(c):
        for q in range(nz):
            arrive(q, c)
        for q in range(nz):
            pair = CH * q + c
            g = q * CH * 2 // per
            at = pair_lanes(pair)
            carried = dot(cv[:, g * N : (g + 1) * N], e_ref[pair].astype(BF16))
            carried = carried * dot(grown[...], spread_ref[:, at])
            out_ref[:, at] = (part[:, at] + carried).astype(BF16)
            y_store(pair).start()

    stages = (
        (each(join, 2), 0), (each(gather, 1), 1), (each(spread_out, 1), 2), (each(send_down, 1), 4),
        (stage_e, 4), (each(pass_on, 2), 6), (stage_d, 6), (stage_f, 7),
    )
    def step(n, carry):
        for stage, after in stages:

            @pl.when(jnp.logical_and(n >= after, n < after + CH))
            def _():
                stage(n - after)

        @pl.when(n < blocks)
        def _():
            block(n)

        @pl.when(n == TABLES)
        def _():
            decode_tables(
                sx_ref, sb_ref, sc_ref, sd_ref, spread_ref, pre_ref, reach_ref, push_ref,
                last_ref, cc_ref, bb_ref,
            )
            for table in tables:
                table.start()

        @pl.when(n >= CLOSE)
        def _():
            close(n - CLOSE)

        return carry

    lax.fori_loop(0, CLOSE + CH, step, 0)

    def drain(c, carry):
        for q in range(nz):
            at_place(q, c, 0, lambda: end_copy(q, c).wait_send())
            at_place(q, c, 3, lambda: far_copy(q, c).wait_send())

            @pl.when(place(q, c) == 1)
            def _():
                for n in range(2):
                    down_copy(q, c, n).wait_send()
                for i in range(1, ny):
                    y_copy(q, c, i).wait_send()
                for l in range(2):
                    for i in range(nz):
                        if i or l:
                            fz_copy(q, c, i, l).wait_send()

                @pl.when(away)
                def _():
                    fz_copy(q, c, 0, 0).wait_send()

            @pl.when(place(q, c) == 2)
            def _():
                join_copy(q, c).wait_send()
                onward_copy(q, c).wait_send()

            y_store(CH * q + c).wait()
        for i in range(1, ny):
            fy_copy(c, i).wait_send()
        for i in range(ny):
            fc_copy(c, i).wait_send()
        g_store(c).wait()
        return carry

    lax.fori_loop(0, CH, drain, 0)
    for table in tables:
        table.wait()


CLOSE = 8
TABLES = 8


def core(x, b, c, decay, sx, sb, sc, sd, nz, ny):
    length, wide = x.shape
    heads = decay.shape[0]
    pairs = heads // 2
    rows = sx.shape[1]
    dma = pltpu.SemaphoreType.DMA
    hbm = pl.BlockSpec(memory_space=pl.ANY)
    pair_shape = (N, 2 * P_SIZE)
    outs = (
        jax.ShapeDtypeStruct(x.shape, BF16),
        jax.ShapeDtypeStruct((CH, ny, 2, 2, nz, 32, N), F32),
        jax.ShapeDtypeStruct((rows, STEPS, wide), F32),
        jax.ShapeDtypeStruct((rows, STEPS, wide), F32),
        jax.ShapeDtypeStruct((wide, 2 * STEPS * rows), BF16),
        jax.ShapeDtypeStruct((rows, heads, N), F32),
        jax.ShapeDtypeStruct((2, rows * STEPS, 2 * N), BF16),
        jax.ShapeDtypeStruct((2, 2 * STEPS * rows, rows * N), BF16),
    )
    return pl.pallas_call(
        functools.partial(core_kernel, (nz, ny)),
        out_shape=outs,
        in_specs=[hbm] * 8,
        out_specs=(hbm,) * len(outs),
        scratch_shapes=[
            pltpu.VMEM(x.shape, BF16),
            pltpu.VMEM(b.shape, BF16),
            pltpu.VMEM(c.shape, BF16),
            pltpu.VMEM(decay.shape, F32),
            pltpu.VMEM(sx.shape, BF16),
            pltpu.VMEM(sb.shape, BF16),
            pltpu.VMEM(sc.shape, BF16),
            pltpu.VMEM(sd.shape, F32),
        ]
        + [pltpu.VMEM(out.shape, out.dtype) for out in outs]
        + [
            pltpu.VMEM((2 * heads, wide), BF16),
            pltpu.VMEM((2, N, length), BF16),
            pltpu.VMEM(x.shape, F32),
            pltpu.VMEM((N, wide), F32),
            pltpu.VMEM((2 * heads, length), F32),
            pltpu.VMEM((length, 2 * heads), F32),
            pltpu.VMEM((length, 2 * heads), BF16),
            pltpu.VMEM((length, 2 * heads), BF16),
            pltpu.VMEM((pairs, N + 8, 2 * P_SIZE), F32),
            pltpu.VMEM((pairs,) + pair_shape, F32),
            pltpu.VMEM((nz, CH, N + 8, 2 * P_SIZE), F32),
            pltpu.VMEM((nz, CH, N + 8, 2 * P_SIZE), F32),
            pltpu.VMEM((nz, CH, 3, N + 8, 2 * P_SIZE), F32),
            pltpu.VMEM((nz, CH, 3) + pair_shape, F32),
            pltpu.VMEM((nz, CH, ny, N + 8, 2 * P_SIZE), F32),
            pltpu.VMEM((nz, CH) + pair_shape, F32),
            pltpu.VMEM((nz, CH) + pair_shape, F32),
            pltpu.VMEM((nz, CH, 2 * P_SIZE, N), F32),
            dma((2 * nz,)),
            dma((7,)),
            dma((pairs,)),
            dma((CH,)),
            dma((6,)),
            dma((nz, CH)), dma((nz, CH)),
            dma((nz, CH)), dma((nz, CH)),
            dma((nz, CH, 3)), dma((nz, CH, 3)),
            dma((nz, CH, 2)), dma((nz, CH)),
            dma((nz, CH, 8)), dma((nz, CH, 2)),
            dma((CH, 3)), dma((CH, 3)),
            dma((CH, 4)), dma((CH, 4)),
        ],
        compiler_params=pltpu.CompilerParams(
            collective_id=0, has_side_effects=True, vmem_limit_bytes=60 * MIB
        ),
        name="core",
    )(x, b, c, decay, sx, sb, sc, sd)


def decode_kernel(
    row_ref, slot_ref, y_hbm, g_hbm, *rest
):
    tables_hbm, rest = rest[:6], rest[6:]
    y_out, out_hbm, cache_hbm, y_ref, g_ref = rest[:5]
    tables, rest = rest[5:11], rest[11:]
    pre_ref, reach_ref, push_ref, last_ref, cc_ref, bb_ref = tables
    out_ref, cache_ref, load_sem, y_load_sem, y_sem, g_sem, out_sem, cache_sem = rest
    rows = pre_ref.shape[0]
    loads = [
        pltpu.make_async_copy(src, dst, load_sem.at[n])
        for n, (src, dst) in enumerate(zip(tables_hbm, tables))
    ]

    def g_load(chunk):
        return pltpu.make_async_copy(g_hbm.at[chunk], g_ref.at[chunk], g_sem.at[chunk])

    height = y_ref.shape[0] // CH

    def y_load(n):
        at = pl.ds(pl.multiple_of(n * height, height), height)
        return pltpu.make_async_copy(y_hbm.at[at], y_ref.at[at], y_load_sem.at[n])

    def y_store(n):
        at = pl.ds(pl.multiple_of(n * height, height), height)
        return pltpu.make_async_copy(y_ref.at[at], y_out.at[at], y_sem.at[n])

    for load in loads:
        load.start()
    g_load(0).start()
    g_load(1).start()
    for n in range(CH):
        y_load(n).start()
    for n in range(2, CH):
        g_load(n).start()
    for load in loads:
        load.wait()

    def cache_store(chunk):
        return pltpu.make_async_copy(
            cache_ref.at[chunk], cache_hbm.at[:, :, chunk], cache_sem.at[chunk]
        )

    def work(chunk, carry):
        y_load(chunk).wait()
        y_store(chunk).start()
        g_load(chunk).wait()
        for zi in range(4):
            g = zi // 2
            pair = CH * zi + chunk
            at = pair_lanes(pair)
            seen = []
            for prompt in range(4):
                f = g_ref[chunk, :, prompt % 2, prompt // 2, zi].reshape(2 * P_SIZE, N)
                hi = f.astype(BF16)
                low = (f - hi.astype(F32)).astype(BF16)
                seen.append(dot(cc_ref[g], jnp.concatenate([hi, low], axis=1), ((1,), (1,))))
            gain = dot(push_ref[at, :], bb_ref[g])
            for r in range(rows):
                mine = row_ref[r]
                part = slice(r * STEPS, (r + 1) * STEPS)
                pick = seen[0][part]
                for prompt in range(1, 4):
                    pick = jnp.where(mine == prompt, seen[prompt][part], pick)
                out_ref[:, r, at] = (pick * reach_ref[r, :, at] + pre_ref[r, :, at]).astype(BF16)
                f = g_ref[chunk, :, mine % 2, mine // 2, zi].reshape(2 * P_SIZE, N)
                kept = jnp.concatenate(
                    [
                        jnp.broadcast_to(last_ref[r, pl.ds(2 * pair + n, 1), :], (P_SIZE, N))
                        for n in range(2)
                    ],
                    axis=0,
                )
                cache_ref[chunk, slot_ref[r], zi] = (
                    f * kept + gain[:, r * N : (r + 1) * N]
                ).astype(BF16)
        cache_store(chunk).start()
        return carry

    lax.fori_loop(0, CH, work, 0)
    out_store = pltpu.make_async_copy(out_ref, out_hbm, out_sem)
    out_store.start()
    for chunk in range(CH):
        y_store(chunk).wait()
        cache_store(chunk).wait()
    out_store.wait()


def decode(row_prompt, cache_slot, y, g, tables, shape):
    rows = shape[1]
    nz = g.shape[4]
    heads = shape[2] // P_SIZE
    smem = pl.BlockSpec(memory_space=pltpu.SMEM)
    hbm = pl.BlockSpec(memory_space=pl.ANY)
    dma = pltpu.SemaphoreType.DMA
    seq, out, cache = pl.pallas_call(
        decode_kernel,
        out_shape=(
            jax.ShapeDtypeStruct(y.shape, BF16),
            jax.ShapeDtypeStruct(shape, BF16),
            jax.ShapeDtypeStruct((rows, nz, CH, 2 * P_SIZE, N), BF16),
        ),
        in_specs=[smem, smem] + [hbm] * (2 + len(tables)),
        out_specs=(hbm, hbm, hbm),
        scratch_shapes=[pltpu.VMEM(a.shape, a.dtype) for a in (y, g, *tables)]
        + [
            pltpu.VMEM(shape, BF16),
            pltpu.VMEM((CH, rows, nz, 2 * P_SIZE, N), BF16),
            dma((len(tables),)),
            dma((CH,)),
            dma((CH,)),
            dma((CH,)),
            dma(()),
            dma((CH,)),
        ],
        compiler_params=pltpu.CompilerParams(vmem_limit_bytes=60 * MIB),
        name="decode",
    )(row_prompt, cache_slot, y, g, *tables)
    return seq, out, cache.reshape(rows, heads, P_SIZE, N)


def per_device(x, b, c, decay, row_prompt, cache_slot, step_x, step_b, step_c, step_decay):
    nz, ny = 4, lax.axis_size("seq") // 4
    y, g, *tables = core(
        x[0], b[0], c[0], decay[0], step_x, step_b, step_c, step_decay, nz, ny
    )
    seq, out, cache = decode(row_prompt, cache_slot, y, g, tables, step_x.shape)
    return seq[None], out, cache


def solution(mesh):
    return jax.shard_map(
        per_device,
        mesh=mesh,
        in_specs=(
            P("tp", "seq", "dp"),
            P("tp", "seq", "dp"),
            P("tp", "seq", "dp"),
            P("tp", "dp", "seq"),
            P(("seq", "dp")),
            P(("seq", "dp")),
            P(None, ("seq", "dp"), "tp"),
            P(None, ("seq", "dp"), "tp"),
            P(None, ("seq", "dp"), "tp"),
            P(None, ("seq", "dp"), "tp"),
        ),
        out_specs=(
            P("tp", "seq", "dp"),
            P(None, ("seq", "dp"), "tp"),
            P(("seq", "dp"), "tp", None, None),
        ),
        check_vma=False,
    )
```

```python
import functools
import math

import jax
import jax.numpy as jnp
from jax import lax
from jax.experimental import pallas as pl
from jax.experimental.pallas import tpu as pltpu
from jax.sharding import PartitionSpec as P

MESH = pl.DeviceIdType.MESH
P_SIZE = 64
N = 128
B = 128
STEPS = 8
LOG2E = math.log2(math.e)
F32 = jnp.float32
BF16 = jnp.bfloat16
CH = 4
MIB = 2**20


def dot(a, b, dims=((1,), (0,)), precision=None):
    return lax.dot_general(
        a, b, (dims, ((), ())), preferred_element_type=F32, precision=precision
    )


def spread_matrix(shape):
    heads = shape[0] // 2
    row = lax.broadcasted_iota(jnp.int32, shape, 0)
    lane = lax.broadcasted_iota(jnp.int32, shape, 1)
    return (row % heads == lane // P_SIZE).astype(F32).astype(BF16)


def pair_lanes(pair):
    return pl.ds(pl.multiple_of(pair * 2 * P_SIZE, 2 * P_SIZE), 2 * P_SIZE)


def hi_low(v):
    hi = v.astype(BF16)
    lane = lax.broadcasted_iota(jnp.int32, v.shape, 1)
    return jnp.where(lane < v.shape[1] // 2, hi, (v - hi.astype(F32)).astype(BF16))


def decode_tables(x_ref, b_ref, c_ref, d_ref, spread_ref, pre_ref, reach_ref, push_ref, last_ref, cc_ref, bb_ref):
    rows, heads = d_ref.shape[1], d_ref.shape[2]
    lane = lax.broadcasted_iota(jnp.int32, (STEPS * STEPS, heads), 1)
    x_all = x_ref[...].astype(F32)
    b_all = b_ref[...].astype(F32)
    c_all = c_ref[...].astype(F32)
    pushes, cs, bs = [], [], []
    for r in range(rows):
        keep = d_ref[:, r, :]
        x, b, c = x_all[:, r, :], b_all[:, r, :], c_all[:, r, :]
        grid = []
        for k in range(STEPS):
            line = [jnp.zeros((1, heads), F32)] * k + [jnp.ones((1, heads), F32)]
            for s in range(k + 1, STEPS):
                line.append(line[-1] * keep[s : s + 1])
            grid.append(jnp.concatenate(line, axis=0))
        line = [keep[0:1]]
        for s in range(1, STEPS):
            line.append(line[-1] * keep[s : s + 1])
        meet = []
        for g in range(2):
            bg, cg = b[:, g * N : (g + 1) * N], c[:, g * N : (g + 1) * N]
            meet.append(
                jnp.concatenate(
                    [jnp.sum(cg * bg[k : k + 1], axis=1, keepdims=True) for k in range(STEPS)],
                    axis=0,
                )
            )
        met = jnp.concatenate(grid, axis=0) * jnp.where(lane < heads // 2, meet[0], meet[1])
        left = [grid[k][STEPS - 1 : STEPS] for k in range(STEPS)]
        table = jnp.concatenate([met] + line + left, axis=0)
        co = dot(hi_low(jnp.concatenate([table, table], axis=1)), spread_ref[...])
        base = STEPS * STEPS
        local = co[0:STEPS] * x[0:1]
        for k in range(1, STEPS):
            local += co[k * STEPS : (k + 1) * STEPS] * x[k : k + 1]
        pre_ref[r] = local
        reach_ref[r] = co[base : base + STEPS]
        push = x * co[base + STEPS : base + 2 * STEPS]
        hi = push.astype(BF16).astype(F32)
        pushes += [hi, push - hi]
        last_ref[r] = jnp.broadcast_to(line[-1], (N, heads)).T
        cs.append(c)
        bs.append(b)
    pushes = jnp.concatenate(pushes, axis=0)
    for pair in range(heads // 2):
        at = pl.ds(pair * 2 * P_SIZE, 2 * P_SIZE)
        push_ref[at, :] = pushes[:, pair * 2 * P_SIZE : (pair + 1) * 2 * P_SIZE].T.astype(BF16)
    cs = jnp.concatenate(cs, axis=0).astype(BF16)
    for g in range(2):
        cg = cs[:, g * N : (g + 1) * N]
        cc_ref[g] = jnp.concatenate([cg, cg], axis=1)
        lines = []
        for r in range(rows):
            b = bs[r][:, g * N : (g + 1) * N]
            zero = jnp.zeros((2 * STEPS, N), F32)
            mine = jnp.concatenate([b, b], axis=0)
            lines.append(
                jnp.concatenate([mine if q == r else zero for q in range(rows)], axis=1)
            )
        bb_ref[g] = jnp.concatenate(lines, axis=0).astype(BF16)


def core_kernel(
    sizes,
    x_hbm,
    b_hbm,
    c_hbm,
    d_hbm,
    sx_hbm,
    sb_hbm,
    sc_hbm,
    sd_hbm,
    out_hbm,
    g_hbm,
    pre_hbm,
    reach_hbm,
    push_hbm,
    last_hbm,
    cc_hbm,
    bb_hbm,
    xv,
    bv,
    cv,
    dv,
    sx_ref,
    sb_ref,
    sc_ref,
    sd_ref,
    out_ref,
    g_ref,
    pre_ref,
    reach_ref,
    push_ref,
    last_ref,
    cc_ref,
    bb_ref,
    spread_ref,
    bt,
    part,
    state,
    cum,
    cum_t,
    grown,
    remain,
    s_ref,
    e_ref,
    first,
    joined,
    ranks,
    starts,
    tops,
    down,
    onward,
    turned,
    x_sem,
    in_sem,
    out_sem,
    g_sem,
    table_sem,
    up_send,
    up_recv,
    join_send,
    join_recv,
    y_send,
    y_recv,
    down_send,
    down_recv,
    fz_send,
    fz_recv,
    fy_send,
    fy_recv,
    fc_send,
    fc_recv,
):
    nz, ny = sizes
    length, wide = xv.shape
    heads = dv.shape[0]
    groups = bv.shape[1] // N
    per = heads // groups
    blocks = length // B
    s, t, d = lax.axis_index("seq"), lax.axis_index("tp"), lax.axis_index("dp")
    y, z = s // nz, s % nz
    zl, core = d // 2, d % 2
    away = t != d

    def x_load(n):
        at = pl.ds(pl.multiple_of(n * 4 * P_SIZE, 4 * P_SIZE), 4 * P_SIZE)
        return pltpu.make_async_copy(x_hbm.at[:, at], xv.at[:, at], x_sem.at[n])

    loads = [
        pltpu.make_async_copy(src, dst, in_sem.at[n])
        for n, (src, dst) in enumerate(
            (
                (d_hbm, dv), (b_hbm, bv), (c_hbm, cv), (sx_hbm, sx_ref), (sb_hbm, sb_ref),
                (sc_hbm, sc_ref), (sd_hbm, sd_ref),
            )
        )
    ]
    tables = [
        pltpu.make_async_copy(src, dst, table_sem.at[n])
        for n, (src, dst) in enumerate(
            (
                (pre_ref, pre_hbm), (reach_ref, reach_hbm), (push_ref, push_hbm),
                (last_ref, last_hbm), (cc_ref, cc_hbm), (bb_ref, bb_hbm),
            )
        )
    ]

    def y_store(pair):
        at = pair_lanes(pair)
        return pltpu.make_async_copy(out_ref.at[:, at], out_hbm.at[:, at], out_sem.at[pair])

    def g_store(c):
        return pltpu.make_async_copy(g_ref.at[c], g_hbm.at[c], g_sem.at[c])

    loads[0].start()
    loads[1].start()
    for half in range(2):
        for q in range(nz):
            x_load(2 * q + half).start()
    for load in loads[2:]:
        load.start()
    spread_ref[...] = spread_matrix(spread_ref.shape)

    def z_dev(i):
        return (y * nz + (z + i) % nz, t, d)

    def y_dev(i):
        return (((y + i) % ny) * nz + z, t, d)

    def cross_dev(i, l):
        return (y * nz + (z + i) % nz, d, (zl + l) % 2 * 2 + t % 2)

    core_dev = (s, t, zl * 2 + 1 - core)

    def own_source(i, p):
        return jnp.logical_and(d == t, p == t // 2) if i == 0 else False

    barrier = pltpu.get_barrier_semaphore()
    others = [z_dev(1), z_dev(nz - 1)] + [y_dev(i) for i in range(1, ny)] + [core_dev]
    for dev in others:
        pl.semaphore_signal(barrier, inc=1, device_id=dev, device_id_type=MESH)
    for i in range(nz):
        for p in range(2):
            prompt = 2 * p + core

            @pl.when(jnp.logical_not(own_source(i, p)))
            def _():
                pl.semaphore_signal(
                    barrier, inc=1, device_id=(y * nz + (z + i) % nz, prompt, t),
                    device_id_type=MESH,
                )


    def copy(src, dst, send, recv, dev):
        return pltpu.make_async_remote_copy(
            src_ref=src, dst_ref=dst, send_sem=send, recv_sem=recv, device_id=dev,
            device_id_type=MESH,
        )

    def turn(q, c):
        return (0, 1, 1 - c % 2, 0)[q]

    def place(q, c):
        j = (z + nz - q) % nz
        return j + turn(q, c) * (3 - 2 * j)

    def near(q, c, step):
        return z_dev(nz + step * (1 - 2 * turn(q, c)))

    def order(q, c):
        f = turn(q, c)
        return ((1, 0, 2), (2, 0, 1), (2 - 2 * f, 1, 2 * f), (0, 2, 1))[q]

    def end_copy(q, c):
        return copy(
            s_ref.at[CH * q + c], ranks.at[q, c, order(q, c)[1]], up_send.at[q, c],
            up_recv.at[q, c], near(q, c, 1),
        )

    def far_copy(q, c):
        return copy(
            s_ref.at[CH * q + c], first.at[q, c], up_send.at[q, c], up_recv.at[q, c],
            near(q, c, -1),
        )

    def join_copy(q, c):
        return copy(
            joined.at[q, c], ranks.at[q, c, order(q, c)[2]], join_send.at[q, c],
            join_recv.at[q, c], near(q, c, -1),
        )

    def y_copy(q, c, i):
        return copy(
            tops.at[q, c, y], tops.at[q, c, y], y_send.at[q, c, i - 1], y_recv.at[q, c, i - 1],
            y_dev(i),
        )

    def down_copy(q, c, n):
        return copy(
            starts.at[q, c, order(q, c)[1 + n]], down.at[q, c], down_send.at[q, c, n],
            down_recv.at[q, c], near(q, c, 2 * n - 1),
        )

    def onward_copy(q, c):
        return copy(
            onward.at[q, c], down.at[q, c], down_send.at[q, c, 0], down_recv.at[q, c],
            near(q, c, 1),
        )

    def fz_copy(q, c, i, l):
        return copy(
            turned.at[q, c, pl.ds(32 * y, 32)], g_ref.at[c, y, t % 2, t // 2, q],
            fz_send.at[q, c, i + nz * l], fz_recv.at[q, c, t // 2], cross_dev(i, l),
        )

    def fz_wait(q, c, p):
        ref = g_ref.at[c, y, core, p, q]
        copy(ref, ref, fz_send.at[q, c, 0], fz_recv.at[q, c, p], core_dev).wait_recv()

    def fy_copy(c, i):
        ref = g_ref.at[c, y, core]
        return copy(ref, ref, fy_send.at[c, i - 1], fy_recv.at[c, i - 1], y_dev(i))

    def fc_copy(c, i):
        ref = g_ref.at[c, (y + ny - i) % ny, core]
        return copy(ref, ref, fc_send.at[c, i], fc_recv.at[c, i], core_dev)

    loads[0].wait()
    row = lax.broadcasted_iota(jnp.int32, (B, B), 0)
    col = lax.broadcasted_iota(jnp.int32, (B, B), 1)
    upper = (row <= col).astype(F32).astype(BF16)
    lead = jnp.zeros((1, 2 * heads), F32)
    leads = []
    rows_of = []
    for k in range(blocks):
        dec = dv[:, k * B : (k + 1) * B] * LOG2E
        hi = dec.astype(BF16)
        mid = (dec - hi.astype(F32)).astype(BF16)
        low = (dec - hi.astype(F32) - mid.astype(F32)).astype(BF16)
        three = jnp.concatenate([hi, mid, low], axis=1)
        rows_of += [three, three]
    sums = dot(jnp.concatenate(rows_of, axis=0), jnp.concatenate([upper] * 3, axis=0))
    for k in range(blocks):
        at = pl.ds(k * B, B)
        mine = sums[k * 2 * heads : (k + 1) * 2 * heads]
        cum[:, at] = mine
        cum_t[at, :] = mine.T
        leads.append(lead)
        lead = lead + cum_t[k * B + B - 1 : k * B + B, :]
    for k in range(blocks):
        at = pl.ds(k * B, B)
        whole = cum_t[at, :] + leads[k]
        remain[at, :] = hi_low(jnp.exp2(jnp.minimum(lead - whole, 0.0)))
    keep = hi_low(jnp.broadcast_to(jnp.exp2(lead), (16, 2 * heads)))

    loads[1].wait()
    for k in range(blocks):
        for g in range(groups):
            at = pl.ds(k * B, B)
            bt[g, :, at] = bv[at, g * N : (g + 1) * N].T

    def at_place(q, c, where, act):
        @pl.when(place(q, c) == where)
        def _():
            act()

    def own_state(half, carry):
        left = remain[...]
        for q in range(nz):
            g = q * CH * 2 // per
            x_load(2 * q + half).wait()
            at = pl.ds(pl.multiple_of((2 * q + half) * 4 * P_SIZE, 4 * P_SIZE), 4 * P_SIZE)
            sp = spread_ref[:, at]
            scaled = (xv[:, at].astype(F32) * dot(left, sp)).astype(BF16)
            both = dot(bt[g], scaled)
            fades = dot(keep, sp)
            for n in range(2):
                c = 2 * half + n
                pair = CH * q + c
                here = slice(n * 2 * P_SIZE, (n + 1) * 2 * P_SIZE)
                s_ref[pair, 0:N] = both[:, here]
                s_ref[pair, N : N + 8] = fades[0:8, here]
                at_place(q, c, 0, lambda: end_copy(q, c).start())
                at_place(q, c, 3, lambda: far_copy(q, c).start())

                @pl.when(place(q, c) == 1)
                def _():
                    ranks[q, c, order(q, c)[0]] = s_ref[pair]

        return carry

    count = len(others) + 2 * nz
    pl.semaphore_wait(barrier, jnp.where(away, count, count - 1))
    lax.fori_loop(0, 2, own_state, 0)
    for load in loads[2:]:
        load.wait()
    for k in range(blocks):
        at = pl.ds(k * B, B)
        grown[at, :] = hi_low(jnp.exp2(cum_t[at, :] + leads[k]))
    state[...] = jnp.zeros((N, wide), F32)
    lane = lax.broadcasted_iota(jnp.int32, (B, 2 * P_SIZE), 1)

    def block(k):
        rows = pl.ds(pl.multiple_of(k * B, B), B)
        sums, sums_t = cum[:, rows], cum_t[rows, :]
        last = sums_t[B - 1 : B, :]
        grow = hi_low(jnp.exp2(sums_t))
        left = hi_low(jnp.exp2(last - sums_t))
        fade = hi_low(jnp.broadcast_to(jnp.exp2(last), (16, 2 * heads)))
        for g in range(groups):
            lanes = pl.ds(g * per * P_SIZE, per * P_SIZE)
            sp = spread_ref[:, lanes]
            c = cv[rows, g * N : (g + 1) * N]
            x = xv[rows, lanes]
            before = state[:, lanes]
            carried = dot(c, before.astype(BF16)) * dot(grow, sp)
            scaled = (x.astype(F32) * dot(left, sp)).astype(BF16)
            term = dot(bt[g, :, rows], scaled)
            state[:, lanes] = before * dot(fade, sp)[0:1, :] + term
            scores = jnp.where(row >= col, dot(c, bt[g, :, rows]), 0.0)
            for n in range(per // 2):
                weights = []
                for h in (g * per + 2 * n, g * per + 2 * n + 1):
                    gap = jnp.minimum(sums_t[:, h : h + 1] - sums[h : h + 1, :], 0.0)
                    weights.append((scores * jnp.exp2(gap)).astype(BF16))
                here = slice(n * 2 * P_SIZE, (n + 1) * 2 * P_SIZE)
                zero = jnp.zeros((B, 2 * P_SIZE), BF16)
                both = jnp.concatenate(
                    [
                        jnp.where(lane < P_SIZE, x[:, here], zero),
                        jnp.where(lane < P_SIZE, zero, x[:, here]),
                    ],
                    axis=0,
                )
                inner = dot(jnp.concatenate(weights, axis=1), both)
                part[rows, pl.ds((g * per + 2 * n) * P_SIZE, 2 * P_SIZE)] = inner + carried[:, here]

    def join(q, c):
        far_copy(q, c).wait_recv()
        pair = CH * q + c
        f = turn(q, c) == 1
        own, other = s_ref[pair, 0:N], first[q, c, 0:N]
        keep, fade = s_ref[pair, N : N + 8], first[q, c, N : N + 8]
        joined[q, c, 0:N] = jnp.where(f, other, own) * jnp.where(f, keep[0:1], fade[0:1]) + (
            jnp.where(f, own, other)
        )
        joined[q, c, N : N + 8] = keep * fade
        join_copy(q, c).start()

    def gather(q, c):
        end_copy(q, c).wait_recv()
        join_copy(q, c).wait_recv()
        top = ranks[q, c, 0, 0:N]
        kept = ranks[q, c, 0, N : N + 8]
        for k in range(1, 3):
            a = ranks[q, c, k, N : N + 8]
            top = top * a[0:1] + ranks[q, c, k, 0:N]
            kept = kept * a
        tops[q, c, y, 0:N] = top
        tops[q, c, y, N : N + 8] = kept
        for i in range(1, ny):
            y_copy(q, c, i).start()

    def spread_out(q, c):
        for i in range(1, ny):
            y_copy(q, c, i).wait_recv()
        enter = jnp.zeros((N, 2 * P_SIZE), F32)
        last = enter
        for k in range(ny):
            a = tops[q, c, k, N : N + 1]
            top = tops[q, c, k, 0:N]
            enter = jnp.where(k < y, enter * a + top, enter)
            last = last * a + top
        turned[q, c] = last.T
        for k in range(3):
            starts[q, c, k] = enter
            if k < 2:
                enter = enter * ranks[q, c, k, N : N + 1] + ranks[q, c, k, 0:N]
        for l in range(2):
            for i in range(nz):
                if i or l:
                    fz_copy(q, c, i, l).start()

        @pl.when(away)
        def _():
            fz_copy(q, c, 0, 0).start()

        @pl.when(jnp.logical_not(away))
        def _():
            g_ref[c, y, core, zl, q] = turned[q, c, pl.ds(32 * y, 32)]

        e_ref[CH * q + c] = starts[q, c, order(q, c)[0]]

    def send_down(q, c):
        for n in (1, 0):
            down_copy(q, c, n).start()

    def pass_on(q, c):
        down_copy(q, c, 1).wait_recv()
        pair = CH * q + c
        f = turn(q, c) == 1
        came = down[q, c]
        own, other = s_ref[pair, 0:N], first[q, c, 0:N]
        a = jnp.where(f, first[q, c, N : N + 1], s_ref[pair, N : N + 1])
        after = came * a + jnp.where(f, other, own)
        onward[q, c] = jnp.where(f, came, after)
        onward_copy(q, c).start()
        e_ref[pair] = jnp.where(f, after, came)

    def arrive(q, c):
        @pl.when(place(q, c) % 3 == 0)
        def _():
            onward_copy(q, c).wait_recv()
            e_ref[CH * q + c] = down[q, c]

    def each(act, where):
        def stage(c):
            for q in range(nz):
                at_place(q, c, where, functools.partial(act, q, c))

        return stage

    def stage_e(c):
        for q in range(nz):
            for p in range(2):
                mine = jnp.logical_and(place(q, c) == 1, jnp.logical_and(d == t, p == t // 2))

                @pl.when(jnp.logical_not(mine))
                def _():
                    fz_wait(q, c, p)

        for i in range(1, ny):
            fy_copy(c, i).start()
        fc_copy(c, 0).start()

    def stage_d(c):
        for i in range(1, ny):
            fy_copy(c, i).wait_recv()
            fc_copy(c, i).start()

    def stage_f(c):
        for i in range(ny):
            fc_copy(c, i).wait_recv()
        g_store(c).start()

    def close(c):
        for q in range(nz):
            arrive(q, c)
        for q in range(nz):
            pair = CH * q + c
            g = q * CH * 2 // per
            at = pair_lanes(pair)
            carried = dot(cv[:, g * N : (g + 1) * N], e_ref[pair].astype(BF16))
            carried = carried * dot(grown[...], spread_ref[:, at])
            out_ref[:, at] = (part[:, at] + carried).astype(BF16)
            y_store(pair).start()

    stages = (
        (each(join, 2), 0), (each(gather, 1), 1), (each(spread_out, 1), 2), (each(send_down, 1), 4),
        (stage_e, 4), (each(pass_on, 2), 5), (stage_d, 6), (stage_f, 7),
    )
    def step(n, carry):
        for stage, after in stages:

            @pl.when(jnp.logical_and(n >= after, n < after + CH))
            def _():
                stage(n - after)

        @pl.when(n < blocks)
        def _():
            block(n)

        @pl.when(n == TABLES)
        def _():
            decode_tables(
                sx_ref, sb_ref, sc_ref, sd_ref, spread_ref, pre_ref, reach_ref, push_ref,
                last_ref, cc_ref, bb_ref,
            )
            for table in tables:
                table.start()

        @pl.when(n >= CLOSE)
        def _():
            close(n - CLOSE)

        return carry

    lax.fori_loop(0, CLOSE + CH, step, 0)

    def drain(c, carry):
        for q in range(nz):
            at_place(q, c, 0, lambda: end_copy(q, c).wait_send())
            at_place(q, c, 3, lambda: far_copy(q, c).wait_send())

            @pl.when(place(q, c) == 1)
            def _():
                for n in range(2):
                    down_copy(q, c, n).wait_send()
                for i in range(1, ny):
                    y_copy(q, c, i).wait_send()
                for l in range(2):
                    for i in range(nz):
                        if i or l:
                            fz_copy(q, c, i, l).wait_send()

                @pl.when(away)
                def _():
                    fz_copy(q, c, 0, 0).wait_send()

            @pl.when(place(q, c) == 2)
            def _():
                join_copy(q, c).wait_send()
                onward_copy(q, c).wait_send()

            y_store(CH * q + c).wait()
        for i in range(1, ny):
            fy_copy(c, i).wait_send()
        for i in range(ny):
            fc_copy(c, i).wait_send()
        g_store(c).wait()
        return carry

    lax.fori_loop(0, CH, drain, 0)
    for table in tables:
        table.wait()


CLOSE = 8
TABLES = 8


def core(x, b, c, decay, sx, sb, sc, sd, nz, ny):
    length, wide = x.shape
    heads = decay.shape[0]
    pairs = heads // 2
    rows = sx.shape[1]
    dma = pltpu.SemaphoreType.DMA
    hbm = pl.BlockSpec(memory_space=pl.ANY)
    pair_shape = (N, 2 * P_SIZE)
    outs = (
        jax.ShapeDtypeStruct(x.shape, BF16),
        jax.ShapeDtypeStruct((CH, ny, 2, 2, nz, 32, N), F32),
        jax.ShapeDtypeStruct((rows, STEPS, wide), F32),
        jax.ShapeDtypeStruct((rows, STEPS, wide), F32),
        jax.ShapeDtypeStruct((wide, 2 * STEPS * rows), BF16),
        jax.ShapeDtypeStruct((rows, heads, N), F32),
        jax.ShapeDtypeStruct((2, rows * STEPS, 2 * N), BF16),
        jax.ShapeDtypeStruct((2, 2 * STEPS * rows, rows * N), BF16),
    )
    return pl.pallas_call(
        functools.partial(core_kernel, (nz, ny)),
        out_shape=outs,
        in_specs=[hbm] * 8,
        out_specs=(hbm,) * len(outs),
        scratch_shapes=[
            pltpu.VMEM(x.shape, BF16),
            pltpu.VMEM(b.shape, BF16),
            pltpu.VMEM(c.shape, BF16),
            pltpu.VMEM(decay.shape, F32),
            pltpu.VMEM(sx.shape, BF16),
            pltpu.VMEM(sb.shape, BF16),
            pltpu.VMEM(sc.shape, BF16),
            pltpu.VMEM(sd.shape, F32),
        ]
        + [pltpu.VMEM(out.shape, out.dtype) for out in outs]
        + [
            pltpu.VMEM((2 * heads, wide), BF16),
            pltpu.VMEM((2, N, length), BF16),
            pltpu.VMEM(x.shape, F32),
            pltpu.VMEM((N, wide), F32),
            pltpu.VMEM((2 * heads, length), F32),
            pltpu.VMEM((length, 2 * heads), F32),
            pltpu.VMEM((length, 2 * heads), BF16),
            pltpu.VMEM((length, 2 * heads), BF16),
            pltpu.VMEM((pairs, N + 8, 2 * P_SIZE), F32),
            pltpu.VMEM((pairs,) + pair_shape, F32),
            pltpu.VMEM((nz, CH, N + 8, 2 * P_SIZE), F32),
            pltpu.VMEM((nz, CH, N + 8, 2 * P_SIZE), F32),
            pltpu.VMEM((nz, CH, 3, N + 8, 2 * P_SIZE), F32),
            pltpu.VMEM((nz, CH, 3) + pair_shape, F32),
            pltpu.VMEM((nz, CH, ny, N + 8, 2 * P_SIZE), F32),
            pltpu.VMEM((nz, CH) + pair_shape, F32),
            pltpu.VMEM((nz, CH) + pair_shape, F32),
            pltpu.VMEM((nz, CH, 2 * P_SIZE, N), F32),
            dma((2 * nz,)),
            dma((7,)),
            dma((pairs,)),
            dma((CH,)),
            dma((6,)),
            dma((nz, CH)), dma((nz, CH)),
            dma((nz, CH)), dma((nz, CH)),
            dma((nz, CH, 3)), dma((nz, CH, 3)),
            dma((nz, CH, 2)), dma((nz, CH)),
            dma((nz, CH, 8)), dma((nz, CH, 2)),
            dma((CH, 3)), dma((CH, 3)),
            dma((CH, 4)), dma((CH, 4)),
        ],
        compiler_params=pltpu.CompilerParams(
            collective_id=0, has_side_effects=True, vmem_limit_bytes=60 * MIB
        ),
        name="core",
    )(x, b, c, decay, sx, sb, sc, sd)


def decode_kernel(
    row_ref, slot_ref, y_hbm, g_hbm, *rest
):
    tables_hbm, rest = rest[:6], rest[6:]
    y_out, out_hbm, cache_hbm, y_ref, g_ref = rest[:5]
    tables, rest = rest[5:11], rest[11:]
    pre_ref, reach_ref, push_ref, last_ref, cc_ref, bb_ref = tables
    out_ref, cache_ref, load_sem, y_load_sem, y_sem, g_sem, out_sem, cache_sem = rest
    rows = pre_ref.shape[0]
    loads = [
        pltpu.make_async_copy(src, dst, load_sem.at[n])
        for n, (src, dst) in enumerate(zip(tables_hbm, tables))
    ]

    def g_load(chunk):
        return pltpu.make_async_copy(g_hbm.at[chunk], g_ref.at[chunk], g_sem.at[chunk])

    height = y_ref.shape[0] // CH

    def y_load(n):
        at = pl.ds(pl.multiple_of(n * height, height), height)
        return pltpu.make_async_copy(y_hbm.at[at], y_ref.at[at], y_load_sem.at[n])

    def y_store(n):
        at = pl.ds(pl.multiple_of(n * height, height), height)
        return pltpu.make_async_copy(y_ref.at[at], y_out.at[at], y_sem.at[n])

    for load in loads:
        load.start()
    g_load(0).start()
    g_load(1).start()
    for n in range(CH):
        y_load(n).start()
    for n in range(2, CH):
        g_load(n).start()
    for load in loads:
        load.wait()

    def cache_store(chunk):
        return pltpu.make_async_copy(
            cache_ref.at[chunk], cache_hbm.at[:, :, chunk], cache_sem.at[chunk]
        )

    def work(chunk, carry):
        y_load(chunk).wait()
        y_store(chunk).start()
        g_load(chunk).wait()
        for zi in range(4):
            g = zi // 2
            pair = CH * zi + chunk
            at = pair_lanes(pair)
            seen = []
            for prompt in range(4):
                f = g_ref[chunk, :, prompt % 2, prompt // 2, zi].reshape(2 * P_SIZE, N)
                hi = f.astype(BF16)
                low = (f - hi.astype(F32)).astype(BF16)
                seen.append(dot(cc_ref[g], jnp.concatenate([hi, low], axis=1), ((1,), (1,))))
            gain = dot(push_ref[at, :], bb_ref[g])
            for r in range(rows):
                mine = row_ref[r]
                part = slice(r * STEPS, (r + 1) * STEPS)
                pick = seen[0][part]
                for prompt in range(1, 4):
                    pick = jnp.where(mine == prompt, seen[prompt][part], pick)
                out_ref[:, r, at] = (pick * reach_ref[r, :, at] + pre_ref[r, :, at]).astype(BF16)
                f = g_ref[chunk, :, mine % 2, mine // 2, zi].reshape(2 * P_SIZE, N)
                kept = jnp.concatenate(
                    [
                        jnp.broadcast_to(last_ref[r, pl.ds(2 * pair + n, 1), :], (P_SIZE, N))
                        for n in range(2)
                    ],
                    axis=0,
                )
                cache_ref[chunk, slot_ref[r], zi] = (
                    f * kept + gain[:, r * N : (r + 1) * N]
                ).astype(BF16)
        cache_store(chunk).start()
        return carry

    lax.fori_loop(0, CH, work, 0)
    out_store = pltpu.make_async_copy(out_ref, out_hbm, out_sem)
    out_store.start()
    for chunk in range(CH):
        y_store(chunk).wait()
        cache_store(chunk).wait()
    out_store.wait()


def decode(row_prompt, cache_slot, y, g, tables, shape):
    rows = shape[1]
    nz = g.shape[4]
    heads = shape[2] // P_SIZE
    smem = pl.BlockSpec(memory_space=pltpu.SMEM)
    hbm = pl.BlockSpec(memory_space=pl.ANY)
    dma = pltpu.SemaphoreType.DMA
    seq, out, cache = pl.pallas_call(
        decode_kernel,
        out_shape=(
            jax.ShapeDtypeStruct(y.shape, BF16),
            jax.ShapeDtypeStruct(shape, BF16),
            jax.ShapeDtypeStruct((rows, nz, CH, 2 * P_SIZE, N), BF16),
        ),
        in_specs=[smem, smem] + [hbm] * (2 + len(tables)),
        out_specs=(hbm, hbm, hbm),
        scratch_shapes=[pltpu.VMEM(a.shape, a.dtype) for a in (y, g, *tables)]
        + [
            pltpu.VMEM(shape, BF16),
            pltpu.VMEM((CH, rows, nz, 2 * P_SIZE, N), BF16),
            dma((len(tables),)),
            dma((CH,)),
            dma((CH,)),
            dma((CH,)),
            dma(()),
            dma((CH,)),
        ],
        compiler_params=pltpu.CompilerParams(vmem_limit_bytes=60 * MIB),
        name="decode",
    )(row_prompt, cache_slot, y, g, *tables)
    return seq, out, cache.reshape(rows, heads, P_SIZE, N)


def per_device(x, b, c, decay, row_prompt, cache_slot, step_x, step_b, step_c, step_decay):
    nz, ny = 4, lax.axis_size("seq") // 4
    y, g, *tables = core(
        x[0], b[0], c[0], decay[0], step_x, step_b, step_c, step_decay, nz, ny
    )
    seq, out, cache = decode(row_prompt, cache_slot, y, g, tables, step_x.shape)
    return seq[None], out, cache


def solution(mesh):
    return jax.shard_map(
        per_device,
        mesh=mesh,
        in_specs=(
            P("tp", "seq", "dp"),
            P("tp", "seq", "dp"),
            P("tp", "seq", "dp"),
            P("tp", "dp", "seq"),
            P(("seq", "dp")),
            P(("seq", "dp")),
            P(None, ("seq", "dp"), "tp"),
            P(None, ("seq", "dp"), "tp"),
            P(None, ("seq", "dp"), "tp"),
            P(None, ("seq", "dp"), "tp"),
        ),
        out_specs=(
            P("tp", "seq", "dp"),
            P(None, ("seq", "dp"), "tp"),
            P(("seq", "dp"), "tp", None, None),
        ),
        check_vma=False,
    )
```
